256 devices in a mesh: section: 8 (over x, core), cache: 32 (over z, y).
Axes of the slice: x: 4, y: 4, z: 8, core: 2. Of those that a mesh axis runs over, the one named last changes fastest.
Arguments:
- hidden_in: bfloat16 [8, 8, 7168], P('section', None, 'cache'), may hold values from -6 to 6
- query_down: bfloat16 [8, 7168, 1536], P('section', 'cache'), may hold values from -0.0625 to 0.0625
- latent_down: bfloat16 [8, 7168, 576], P('section', 'cache'), may hold values from -0.0625 to 0.0625
- query_gain: float32 [8, 1536], P('section'), may hold values from 0.1 to 1.9
- latent_gain: float32 [8, 512], P('section'), may hold values from 0.25 to 4
- query_up: bfloat16 [8, 1536, 36864], P('section', None, 'cache'), may hold values from -0.15625 to 0.15625
- value_up: bfloat16 [8, 64, 512, 128], P('section', 'cache'), may hold values from -0.25 to 0.25
- output_proj: bfloat16 [8, 8192, 7168], P('section', 'cache'), may hold values from -0.5 to 0.5
- latent_cache: bfloat16 [8, 8, 8192, 576], P('section', None, 'cache'), may hold values from -70 to 70
- selected: int32 [8, 8, 32], P('section'), may hold values from 0 to 127, as said below
- lengths: int32 [8, 8], P('section'), may hold values from 2048 to 8192, as said below
Outputs:
- arrived: float32 [8, 8, 7168], P('section', None, 'cache')
The draws below stay inside these ranges and needn't reach their ends.
Inputs may be any that keep to these rules, and one draw needn't show every extreme that they name: `selected`: each row names 32 different blocks, all below ceil(length / 64), among them the block holding position length - 1. `lengths`: the first sequence of every layer has all 8192 positions.
All inputs are finite; a program needn't handle non-finite values.
Results may differ from the reference program's by a relative error of at most 0.019.
Values may be sent and summed in bfloat16 or wider, within the bound.
A program may use at most 128 MiB of HBM per device.

```python
import math
import jax
import jax.numpy as jnp
from jax import lax

D = 7168
QL = 1536
LAT = 512
ROPE = 64
HV = 128
H = 64
BLK = 64
TOPB = 32
SEQ = 8
KW = 576
NBLK = 128
LEN = 8192
N_SECTION = 8


def choose_blocks(key):
    length_key, order_key = jax.random.split(key)
    seq_lengths = jax.random.randint(length_key, (N_SECTION, SEQ), TOPB * BLK, LEN + 1)
    seq_lengths = seq_lengths.at[:, 0].set(LEN)
    row_keys = jax.random.split(order_key, N_SECTION * SEQ)
    ranks = jax.vmap(lambda one: jax.random.permutation(one, NBLK))(row_keys).reshape(N_SECTION, SEQ, NBLK)
    usable = (seq_lengths + BLK - 1) // BLK
    block_ids = jnp.arange(NBLK, dtype=jnp.int32)[None, None, :]
    ranks = jnp.where(block_ids < usable[:, :, None], ranks, ranks + NBLK)
    ranks = jnp.where(block_ids == usable[:, :, None] - 1, -1, ranks)
    order = jnp.argsort(ranks, axis=-1, stable=True)[:, :, :TOPB]
    return (seq_lengths.astype(jnp.int32), order.astype(jnp.int32))


def draw_selected(key, part):
    return choose_blocks(key)[1]


def draw_lengths(key, part):
    return choose_blocks(key)[0]


def draw_latent_cache(key, part):
    key = jax.random.fold_in(key, 7)
    base_key = jax.random.fold_in(key, 0)
    shape = (N_SECTION, SEQ, LEN, KW)
    return jnp.clip(jax.random.normal(base_key, shape, jnp.float32), -6.0, 6.0).astype(jnp.bfloat16)


def steps_of(stream_key, dims, shards, low, largest):
    level = 1.0
    for dim, blocks in shards:
        heights = jax.random.uniform(jax.random.fold_in(jax.random.fold_in(stream_key, 6), dim), (blocks,), jnp.float32, low / len(shards), largest / len(shards))
        level = level * jnp.repeat(jnp.exp(heights), dims[dim] // blocks).reshape((-1,) + (1,) * (len(dims) - 1 - dim))
    return level


def noise(key, dims, spread, limit, cuts=(), held_as=jnp.bfloat16):
    result = jax.random.normal(key, dims, jnp.float32) * spread
    if len(cuts) > 0:
        result = steps_of(key, dims, cuts, -0.22, 0.18) * result
    return jnp.clip(result, min=-limit, max=limit).astype(held_as)


def setup_inputs(seed: int = 0) -> dict:
    key_of = jax.random.split(jax.random.key(seed), 12)
    return {
        "hidden_in": noise(key_of[0], (N_SECTION, SEQ, D), 1.0, 6.0, ((0, 8), (2, 32))),
        "query_down": noise(key_of[1], (N_SECTION, D, QL), D ** -0.5, 0.0625, ((0, 8), (1, 32))),
        "latent_down": noise(key_of[2], (N_SECTION, D, KW), D ** -0.5, 0.0625, ((0, 8), (1, 32))),
        "query_gain": jnp.clip(1.0 + 0.18 * jax.random.normal(key_of[3], (N_SECTION, QL), jnp.float32), 0.1, 1.9),
        "latent_gain": jnp.clip(jnp.exp(math.log(4.0) - 2.7725887 * jax.random.uniform(key_of[4], (N_SECTION, LAT), jnp.float32) ** steps_of(key_of[4], (N_SECTION, LAT), ((0, 8),), -0.2, 0.2)), 0.25, 4.0),
        "query_up": noise(key_of[5], (N_SECTION, QL, H * KW), QL ** -0.5, 0.15625, ((0, 8), (2, 32))),
        "value_up": noise(key_of[6], (N_SECTION, H, LAT, HV), LAT ** -0.5, 0.25, ((0, 8), (1, 32))),
        "output_proj": noise(key_of[7], (N_SECTION, H * HV, D), (H * HV // 64) ** -0.5, 0.5, ((0, 8), (1, 32))),
        "latent_cache": draw_latent_cache(jax.random.fold_in(key_of[11], 71), 0),
        "selected": draw_selected(jax.random.fold_in(key_of[11], 71), 0),
        "lengths": draw_lengths(jax.random.fold_in(key_of[11], 71), 0),
    }


def rms_scale(values):
    return values * lax.rsqrt(lax.optimization_barrier(jnp.mean(values * values, axis=-1, keepdims=True)) + 1e-06)

def one_layer(operands):
    hidden_row, q_down, kv_down, q_gain, kv_gain, q_up, v_up, o_proj, cache_rows, chosen_ids, seq_len = operands
    query_lat = jnp.dot(hidden_row, q_down, preferred_element_type=jnp.float32)
    kv_new = jnp.dot(hidden_row, kv_down, preferred_element_type=jnp.float32)
    query_norm = (rms_scale(query_lat) * q_gain).astype(jnp.bfloat16)
    new_lat = rms_scale(kv_new[:, :LAT]) * kv_gain
    new_key = jnp.concatenate([new_lat, kv_new[:, LAT:]], axis=1).astype(jnp.bfloat16)
    queries = jnp.dot(query_norm, q_up, preferred_element_type=jnp.float32).astype(jnp.bfloat16)
    queries = queries.reshape(SEQ, H, KW).astype(jnp.float32)
    blocks = cache_rows.reshape(SEQ, NBLK, BLK, KW)
    picked = jnp.take_along_axis(blocks, chosen_ids[:, :, None, None].astype(jnp.int32), axis=1)
    picked = picked.reshape(SEQ, TOPB * BLK, KW).astype(jnp.float32)
    position = (chosen_ids[:, :, None] * BLK + jnp.arange(BLK, dtype=jnp.int32)[None, None, :]).reshape(SEQ, TOPB * BLK)
    valid = position < seq_len[:, None]
    scale = (HV + ROPE) ** (-0.5)
    scores = jnp.einsum('bhk,bpk->bhp', queries, picked) * scale
    scores = jnp.where(valid[:, None, :], scores, -1e+30)
    new_score = jnp.einsum('bhk,bk->bh', queries, new_key.astype(jnp.float32)) * scale
    top = jnp.maximum(lax.optimization_barrier(jnp.max(scores, axis=-1)), new_score)
    expo = jnp.where(valid[:, None, :], jnp.exp(scores - top[:, :, None]), 0.0)
    new_expo = jnp.exp(new_score - top)
    total = lax.optimization_barrier(jnp.sum(expo, axis=-1)) + new_expo
    weights = expo.astype(jnp.bfloat16).astype(jnp.float32)
    new_weight = new_expo.astype(jnp.bfloat16).astype(jnp.float32)
    summed = jnp.einsum('bhp,bpc->bhc', weights, picked[:, :, :LAT])
    summed = summed + new_weight[:, :, None] * new_key[:, None, :LAT].astype(jnp.float32)
    attended = (summed / total[:, :, None]).astype(jnp.bfloat16)
    head_out = jnp.einsum('bhc,hcv->bhv', attended.astype(jnp.float32), v_up.astype(jnp.float32)).astype(jnp.bfloat16)
    head_out = head_out.reshape(SEQ, H * HV)
    layer_out = jnp.dot(head_out, o_proj, preferred_element_type=jnp.float32) + hidden_row.astype(jnp.float32)
    return layer_out

def reference(hidden_in, query_down, latent_down, query_gain, latent_gain, query_up, value_up, output_proj, latent_cache, selected, lengths):
    outputs = lax.map(one_layer, (hidden_in, query_down, latent_down, query_gain, latent_gain, query_up, value_up, output_proj, latent_cache, selected, lengths))
    return jnp.roll(outputs, 1, axis=0)
```

```python
import functools

import jax
import jax.numpy as jnp
from jax import lax
from jax.experimental import pallas as pl
from jax.experimental.pallas import tpu as pltpu
from jax.sharding import PartitionSpec as P

MESH = pl.DeviceIdType.MESH
F32 = jnp.float32
BF16 = jnp.bfloat16

SEQ = 8
QL = 1536
LAT = 512
ROPE = 64
HV = 128
BLK = 64
KW = 576
PADKW = 640
NZ = 8
NY = 4
NC = NZ * NY
NSEC = 8
FEAT = 224
POS = 256
QT = QL // 128
KT = LAT // 128
TILES = QT + KT + 1
SCALE = (HV + ROPE) ** (-0.5)
NEAR_FIRST = (1, 7, 2, 6, 3, 5, 4)
FAR_FIRST = (4, 3, 5, 2, 6, 1, 7, 0)


def split_three(value):
    high = value.astype(BF16).astype(F32)
    rest = value - high
    middle = rest.astype(BF16).astype(F32)
    return high, middle, rest - middle


def two_rows(value):
    high = value.astype(BF16)
    low = (value - high.astype(F32)).astype(BF16)
    return jnp.concatenate([high.astype(F32), low.astype(F32)], axis=0).astype(BF16)


def with_stats(summed, top, total):
    lane = lax.broadcasted_iota(jnp.int32, (summed.shape[0], 128), 1)
    stats = jnp.zeros((summed.shape[0], 128), F32)
    for at, piece in enumerate(split_three(top) + split_three(total)):
        stats = jnp.where(lane == at, piece, stats)
    return jnp.concatenate([summed, stats], axis=1)


def parts_of(block):
    stats = block[:, LAT:]
    lane = lax.broadcasted_iota(jnp.int32, stats.shape, 1)
    top = jnp.sum(jnp.where(lane < 3, stats, 0.0), axis=1, keepdims=True)
    total = jnp.sum(jnp.where((lane >= 3) & (lane < 6), stats, 0.0), axis=1, keepdims=True)
    return block[:, :LAT], top, total


def merged(parts):
    top = functools.reduce(jnp.maximum, [p[1] for p in parts])
    scales = [jnp.exp(p[1] - top) for p in parts]
    total = functools.reduce(jnp.add, [p[2] * a for p, a in zip(parts, scales)])
    summed = functools.reduce(jnp.add, [p[0] * a for p, a in zip(parts, scales)])
    return summed, top, total


def kernel(
    hidden,
    query_down,
    latent_down,
    query_gain,
    latent_gain,
    query_up,
    value_up,
    output_proj,
    latent_cache,
    selected,
    lengths,
    out,
    qd,
    ld,
    qu,
    vu,
    op,
    kv,
    part,
    rs_in,
    lat,
    q_all,
    q_f32,
    o_f32,
    o_out,
    y_in,
    c_out,
    z_in,
    e_out,
    e_in,
    x_out,
    x_in,
    load_sem,
    send_sem,
    x_sem,
    rs_sem,
    ag_sem,
    qz_sem,
    qy_sem,
    dy_sem,
    dz_sem,
    e_sem,
    next_sem,
):
    sec = lax.axis_index("section")
    me = lax.axis_index("cache")
    z = me // NY
    y = me % NY
    after = lax.rem(sec + 1, NSEC)
    before = lax.rem(sec + NSEC - 1, NSEC)

    def at(dz, dy):
        return lax.rem(z + dz, NZ) * NY + lax.rem(y + dy, NY)

    def load(source, target, index):
        copy = pltpu.make_async_copy(source, target, load_sem.at[index])
        copy.start()
        return copy

    def send(source, target, send_index, recv, device):
        pltpu.make_async_remote_copy(
            src_ref=source,
            dst_ref=target,
            send_sem=send_sem.at[send_index],
            recv_sem=recv,
            device_id=device,
            device_id_type=MESH,
        ).start()

    def wait_bytes(ref, sem):
        pltpu.make_async_copy(ref, ref, sem).wait()

    qd_load = load(query_down.at[0], qd, 0)
    ld_load = load(latent_down.at[0], ld, 1)

    barrier = pltpu.get_barrier_semaphore()

    @pl.loop(1, NC)
    def _(d):
        pl.semaphore_signal(
            barrier, inc=1, device_id={"cache": lax.rem(me + d, NC)}, device_id_type=MESH
        )

    for other in (after, before):
        pl.semaphore_signal(barrier, inc=1, device_id={"section": other}, device_id_type=MESH)

    qu_load = load(query_up.at[0], qu, 2)
    kv_load = load(latent_cache.at[0], kv, 3)
    vu_load = load(value_up.at[0], vu, 4)
    op_load = load(output_proj.at[0], op, 5)

    rows = hidden[0]
    qd_load.wait()
    part_q = jnp.dot(rows, qd[...], preferred_element_type=F32)
    for t in range(QT):
        part[t] = part_q[:, t * 128 : (t + 1) * 128]
    ld_load.wait()
    part_kv = jnp.dot(rows, ld[...], preferred_element_type=F32)
    for t in range(KT):
        part[QT + t] = part_kv[:, t * 128 : (t + 1) * 128]
    empty = jnp.zeros((SEQ, 128 - ROPE), F32)
    part[QT + KT] = jnp.concatenate([part_kv[:, LAT:], empty], axis=1)
    own_rows = rows.astype(F32)
    right_rows = jnp.concatenate([own_rows[:, 128:], jnp.zeros((SEQ, 32), F32)], axis=1)
    x_out[...] = jnp.concatenate([own_rows[:, :128], right_rows], axis=0).astype(BF16)

    pl.semaphore_wait(barrier, NC + 1)
    pl.semaphore_signal(next_sem, inc=1, device_id={"section": before}, device_id_type=MESH)

    is_owner = (lax.rem(me, 2) == 0) | (me == 1)
    my_tile = jnp.where(me == 1, TILES - 1, me // 2)

    @pl.loop(0, TILES)
    def _(t):
        owner = jnp.where(t == TILES - 1, 1, 2 * t)

        @pl.when(owner != me)
        def _():
            slot = lax.rem(owner - me + NC, NC) - 1
            send(part.at[t], rs_in.at[slot], 0, rs_sem, {"cache": owner})

    send(x_out, x_in, 1, x_sem, {"section": after})

    @pl.when(is_owner)
    def _():
        wait_bytes(rs_in, rs_sem)
        total = part[my_tile]
        for slot in range(NC - 1):
            total = total + rs_in[slot]
        lat[my_tile] = total

        @pl.loop(1, NC)
        def _(d):
            send(lat.at[my_tile], lat.at[my_tile], 2, ag_sem, {"cache": lax.rem(me + d, NC)})

        wait_bytes(lat.at[pl.ds(0, TILES - 1)], ag_sem)

    @pl.when(jnp.logical_not(is_owner))
    def _():
        wait_bytes(lat, ag_sem)

    squares = lat[0] * lat[0]
    for t in range(1, QT):
        squares = squares + lat[t] * lat[t]
    mean = jnp.sum(squares, axis=1, keepdims=True) * (1.0 / QL)
    q_scale = lax.rsqrt(mean + 1e-06)
    query_norm = jnp.concatenate(
        [lat[t] * q_scale * query_gain[0:1, t * 128 : (t + 1) * 128] for t in range(QT)], axis=1
    ).astype(BF16)
    qu_load.wait()
    own = jnp.dot(query_norm, qu[...], preferred_element_type=F32)
    first = own[:, :PADKW]
    second = pltpu.roll(own[:, LAT:], PADKW - ROPE, axis=1)
    own_q = jnp.concatenate([first, second], axis=0).astype(BF16)
    q_all[0] = own_q

    for dz in (4, 3, 5, 2, 6, 1, 7):
        slot = (NZ - dz) * NY
        send(q_all.at[0], q_all.at[slot], 3, qz_sem.at[NZ - dz], {"cache": at(dz, 0)})
    for dy in (2, 1, 3):
        send(q_all.at[0], q_all.at[NY - dy], 4, qy_sem, {"cache": at(0, dy)})

    squares = lat[QT] * lat[QT]
    for t in range(1, KT):
        squares = squares + lat[QT + t] * lat[QT + t]
    mean = jnp.sum(squares, axis=1, keepdims=True) * (1.0 / LAT)
    kv_scale = lax.rsqrt(mean + 1e-06)
    new_key = jnp.concatenate(
        [
            lat[QT + t] * kv_scale * latent_gain[0:1, t * 128 : (t + 1) * 128]
            for t in range(KT)
        ]
        + [lat[QT + KT]],
        axis=1,
    )
    new_key = new_key.astype(BF16).astype(F32)
    new_key = jnp.concatenate([new_key, new_key], axis=0)
    new_score = jnp.sum(own_q.astype(F32) * new_key, axis=1, keepdims=True) * SCALE

    chosen = selected[0]
    lane = lax.broadcasted_iota(jnp.int32, (SEQ, POS), 1)
    hits = jnp.zeros((SEQ, POS), F32)
    for j in range(POS // BLK):
        hit = jnp.where(chosen == me * (POS // BLK) + j, 1.0, 0.0)
        hit = jnp.max(hit, axis=1, keepdims=True)
        hits = jnp.where(lane // BLK == j, hit, hits)
    position = lax.broadcasted_iota(jnp.int32, (1, POS), 1) + me * POS

    for r in NEAR_FIRST:
        block = q_all.at[r * NY]
        wait_bytes(block, qz_sem.at[r])
        for dy in (2, 1, 3):
            send(block, q_all.at[r * NY + NY - dy], 4, qy_sem, {"cache": at(0, dy)})
    wait_bytes(q_all.at[pl.ds(0, NC - NZ)], qy_sem)

    for r in range(NZ):
        for dy in range(NY):
            block = r * NY + dy
            wide = q_all[block].astype(F32)
            for t in range(KT + 1):
                q_f32[t, block * 16 : block * 16 + 16, :] = wide[:, t * 128 : (t + 1) * 128]

    kv_load.wait()
    for b in range(SEQ):
        queries = jnp.concatenate(
            [q_f32[t, pl.ds(b, 64, stride=SEQ), :] for t in range(KT + 1)], axis=1
        )
        queries = queries[:, :KW].astype(BF16)
        keys = kv[b]
        scores = (
            jnp.dot(queries, keys, preferred_element_type=F32) * SCALE
        )
        valid = (hits[b : b + 1, :] > 0.5) & (position < lengths[0, b])
        masked = jnp.where(valid, scores, -1e30)
        top = jnp.max(masked, axis=1, keepdims=True)
        expo = jnp.where(valid, jnp.exp(masked - top), 0.0)
        total = jnp.sum(expo, axis=1, keepdims=True)
        summed = lax.dot_general(
            expo.astype(BF16),
            keys[:LAT],
            (((1,), (1,)), ((), ())),
            preferred_element_type=F32,
        )
        wide = with_stats(summed, top, total)
        for t in range(KT + 1):
            o_f32[t, pl.ds(b, 64, stride=SEQ), :] = wide[:, t * 128 : (t + 1) * 128]

    def own_block(block):
        return jnp.concatenate(
            [o_f32[t, block * 16 : block * 16 + 16, :] for t in range(KT + 1)], axis=1
        )

    for r in FAR_FIRST:
        for dy in (2, 1, 3):
            block = r * NY + dy
            o_out[block] = own_block(block).astype(BF16)
            send(o_out.at[block], y_in.at[r, NY - 1 - dy], 5, dy_sem.at[r], {"cache": at(0, dy)})
    for r in FAR_FIRST:
        wait_bytes(y_in.at[r], dy_sem.at[r])
        parts = [parts_of(own_block(r * NY))]
        parts += [parts_of(y_in[r, k].astype(F32)) for k in range(NY - 1)]
        joined = merged(parts)
        if r > 0:
            c_out[r - 1] = with_stats(*joined).astype(BF16)
            send(c_out.at[r - 1], z_in.at[NZ - 1 - r], 6, dz_sem, {"cache": at(r, 0)})
    wait_bytes(z_in, dz_sem)
    parts = [joined, (new_key[:, :LAT], new_score, jnp.ones((2 * SEQ, 1), F32))]
    parts += [parts_of(z_in[k].astype(F32)) for k in range(NZ - 1)]
    summed, _, total = merged(parts)
    attended = summed / total

    vu_load.wait()
    heads = []
    for h in range(2):
        both = two_rows(attended[h * SEQ : (h + 1) * SEQ, :])
        value = jnp.dot(both, vu[h], preferred_element_type=F32)
        heads.append(value[:SEQ] + value[SEQ:])
    head_out = two_rows(jnp.concatenate(heads, axis=1))
    op_load.wait()
    pl.semaphore_wait(next_sem, 1)
    width = NY * FEAT
    for r in FAR_FIRST:
        zt = lax.rem(z + r, NZ)
        columns = op[:, pl.ds(pl.multiple_of(zt * width, 128), width)]
        both = jnp.dot(head_out, columns, preferred_element_type=F32)
        projected = both[:SEQ] + both[SEQ:]
        for k in range(NY):
            start = k * FEAT // 128 * 128
            shift = k * FEAT - start
            stop = -(-(k * FEAT + FEAT) // 128) * 128
            piece = projected[:, start:stop]
            if shift:
                piece = pltpu.roll(piece, stop - start - shift, axis=1)
            block = jnp.concatenate([piece[:, :128], piece[:, 128:256]], axis=0)
            e_out[r * NY + k] = block.astype(BF16)
            slot = (NZ - r) % NZ * NY + y
            send(
                e_out.at[r * NY + k],
                e_in.at[slot],
                7,
                e_sem,
                {"section": after, "cache": zt * NY + k},
            )

    wait_bytes(x_in, x_sem)
    total = x_in[...].astype(F32)
    wait_bytes(e_in, e_sem)
    for slot in range(NC):
        total = total + e_in[slot].astype(F32)
    out[0, :, :128] = total[:SEQ]
    out[0, :, 128:] = total[SEQ:, : FEAT - 128]

    @pl.when(is_owner)
    def _():
        wait_bytes(part.at[pl.ds(0, TILES - 1)], send_sem.at[0])
        wait_bytes(rs_in, send_sem.at[2])

    @pl.when(jnp.logical_not(is_owner))
    def _():
        wait_bytes(part, send_sem.at[0])

    wait_bytes(x_out, send_sem.at[1])
    wait_bytes(q_all.at[pl.ds(0, NZ - 1)], send_sem.at[3])
    wait_bytes(q_all.at[pl.ds(0, NC - NZ)], send_sem.at[4])
    wait_bytes(o_out.at[pl.ds(0, NC - NZ)], send_sem.at[5])
    wait_bytes(c_out, send_sem.at[6])
    wait_bytes(e_out, send_sem.at[7])


def on_device(*arrays):
    arrays = list(arrays)
    arrays[8] = jnp.swapaxes(arrays[8], 2, 3)
    vmem = pl.BlockSpec(memory_space=pltpu.VMEM)
    smem = pl.BlockSpec(memory_space=pltpu.SMEM)
    hbm = pl.BlockSpec(memory_space=pl.ANY)
    dma = pltpu.SemaphoreType.DMA
    return pl.pallas_call(
        kernel,
        out_shape=jax.ShapeDtypeStruct((1, SEQ, FEAT), F32),
        in_specs=[vmem, hbm, hbm, vmem, vmem, hbm, hbm, hbm, hbm, vmem, smem],
        out_specs=vmem,
        scratch_shapes=[
            pltpu.VMEM((FEAT, QL), BF16),
            pltpu.VMEM((FEAT, KW), BF16),
            pltpu.VMEM((QL, 2 * KW), BF16),
            pltpu.VMEM((2, LAT, HV), BF16),
            pltpu.VMEM((2 * HV, NC * FEAT), BF16),
            pltpu.VMEM((SEQ, KW, POS), BF16),
            pltpu.VMEM((TILES, SEQ, 128), F32),
            pltpu.VMEM((NC - 1, SEQ, 128), F32),
            pltpu.VMEM((TILES, SEQ, 128), F32),
            pltpu.VMEM((NC, 16, PADKW), BF16),
            pltpu.VMEM((KT + 1, NC * 16, 128), F32),
            pltpu.VMEM((KT + 1, NC * 16, 128), F32),
            pltpu.VMEM((NC, 16, PADKW), BF16),
            pltpu.VMEM((NZ, NY - 1, 16, PADKW), BF16),
            pltpu.VMEM((NZ - 1, 16, PADKW), BF16),
            pltpu.VMEM((NZ - 1, 16, PADKW), BF16),
            pltpu.VMEM((NC, 16, 128), BF16),
            pltpu.VMEM((NC, 16, 128), BF16),
            pltpu.VMEM((16, 128), BF16),
            pltpu.VMEM((16, 128), BF16),
            dma((6,)),
            dma((8,)),
            dma,
            dma,
            dma,
            dma((NZ,)),
            dma,
            dma((NZ,)),
            dma,
            dma,
            pltpu.SemaphoreType.REGULAR,
        ],
        compiler_params=pltpu.CompilerParams(
            collective_id=0, has_side_effects=True, vmem_limit_bytes=60 << 20
        ),
        cost_estimate=pl.CostEstimate(
            flops=400_000_000, bytes_accessed=11_000_000, transcendentals=200_000
        ),
    )(*arrays)


def solution(mesh):
    return jax.shard_map(
        on_device,
        mesh=mesh,
        in_specs=(
            P("section", None, "cache"),
            P("section", "cache", None),
            P("section", "cache", None),
            P("section", None),
            P("section", None),
            P("section", None, "cache"),
            P("section", "cache", None, None),
            P("section", "cache", None),
            P("section", None, "cache", None),
            P("section", None, None),
            P("section", None),
        ),
        out_specs=P("section", None, "cache"),
        check_vma=False,
    )
```

```python
import functools

import jax
import jax.numpy as jnp
from jax import lax
from jax.experimental import pallas as pl
from jax.experimental.pallas import tpu as pltpu
from jax.sharding import PartitionSpec as P

MESH = pl.DeviceIdType.MESH
F32 = jnp.float32
BF16 = jnp.bfloat16

SEQ = 8
QL = 1536
LAT = 512
ROPE = 64
HV = 128
BLK = 64
KW = 576
PADKW = 640
NZ = 8
NY = 4
NC = NZ * NY
NSEC = 8
FEAT = 224
POS = 256
QT = QL // 128
KT = LAT // 128
SCALE = (HV + ROPE) ** (-0.5)
ORDER = (0, 1, 7, 2, 6, 3, 5, 4)
GROUPS = (ORDER[:4], ORDER[4:])
GROUP_OF = {r: g for g, group in enumerate(GROUPS) for r in group}
SEND_ORDER = ((2, 7, 1, 0), (4, 5, 3, 6))
FAR_FIRST = (4, 3, 5, 2, 6, 1, 7, 0)
HALF = 4 * NY * 16


def split_three(value):
    high = value.astype(BF16).astype(F32)
    rest = value - high
    middle = rest.astype(BF16).astype(F32)
    return high, middle, rest - middle


def two_rows(value):
    high = value.astype(BF16)
    low = (value - high.astype(F32)).astype(BF16)
    return jnp.concatenate([high.astype(F32), low.astype(F32)], axis=0).astype(BF16)


def folded(value):
    half = value.shape[0] // 2
    return value[:half] + value[half:]


def stats_tile(top, total, places=0):
    lane = lax.broadcasted_iota(jnp.int32, (top.shape[0], 128), 1) - places
    stats = jnp.zeros((top.shape[0], 128), F32)
    for at, piece in enumerate(split_three(top) + split_three(total)):
        stats = jnp.where(lane == at, piece, stats)
    return stats


def read_stats(stats, place=0):
    lane = lax.broadcasted_iota(jnp.int32, stats.shape, 1) - place
    top = jnp.where((lane >= 0) & (lane < 3), stats, 0.0)
    total = jnp.where((lane >= 3) & (lane < 6), stats, 0.0)
    return jnp.sum(top, axis=1, keepdims=True), jnp.sum(total, axis=1, keepdims=True)


def merged(parts):
    top = functools.reduce(jnp.maximum, [p[1] for p in parts])
    scales = [jnp.exp(p[1] - top) for p in parts]
    total = functools.reduce(jnp.add, [p[2] * a for p, a in zip(parts, scales)])
    summed = functools.reduce(jnp.add, [p[0] * a for p, a in zip(parts, scales)])
    return summed, top, total


def kernel(
    hidden,
    query_down,
    latent_down,
    query_gain,
    latent_gain,
    query_up,
    value_up,
    output_proj,
    latent_cache,
    selected,
    lengths,
    out,
    hid,
    qgain,
    lgain,
    chosen,
    limits,
    qd,
    ld,
    qu,
    vu,
    op,
    kv,
    part_q,
    part_k,
    y_q,
    y_k,
    own_qs,
    own_ks,
    z_q,
    z_k,
    lat_q,
    lat_k,
    q_all,
    q_rope,
    q_f32,
    o_f32,
    s_f32,
    o_out,
    s_out,
    y_in,
    ys_in,
    c_out,
    z_in,
    e_out,
    e_in,
    x_out,
    x_in,
    load_sem,
    send_sem,
    recv_sem,
    qz_sem,
    qy_sem,
    rope_sem,
    dy_sem,
    ds_sem,
    next_sem,
):
    sec = lax.axis_index("section")
    me = lax.axis_index("cache")
    z = me // NY
    y = me % NY
    after = lax.rem(sec + 1, NSEC)
    before = lax.rem(sec + NSEC - 1, NSEC)

    def at(dz, dy):
        return {"cache": lax.rem(z + dz, NZ) * NY + lax.rem(y + dy, NY)}

    def load(source, target, index):
        copy = pltpu.make_async_copy(source, target, load_sem.at[index])
        copy.start()
        return copy

    def send(source, target, send_index, recv, device):
        pltpu.make_async_remote_copy(
            src_ref=source,
            dst_ref=target,
            send_sem=send_sem.at[send_index],
            recv_sem=recv,
            device_id=device,
            device_id_type=MESH,
        ).start()

    def wait_bytes(ref, sem):
        pltpu.make_async_copy(ref, ref, sem).wait()

    barrier = pltpu.get_barrier_semaphore()
    for dz in (4, 3, 5, 2, 6, 1, 7):
        pl.semaphore_signal(barrier, inc=1, device_id=at(dz, 0), device_id_type=MESH)
    for dy in (2, 1, 3):
        pl.semaphore_signal(barrier, inc=1, device_id=at(0, dy), device_id_type=MESH)
    for other in (after, before):
        pl.semaphore_signal(barrier, inc=1, device_id={"section": other}, device_id_type=MESH)

    hid_load = load(hidden.at[0], hid, 0)
    qd_load = load(query_down.at[0], qd, 1)
    ld_load = load(latent_down.at[0], ld, 2)
    qgain_load = load(query_gain, qgain, 3)
    lgain_load = load(latent_gain, lgain, 4)
    chosen_load = load(selected.at[0], chosen, 5)
    limits_load = load(lengths, limits, 6)
    qu_load = load(query_up.at[0], qu, 7)
    kv_load = load(latent_cache.at[0], kv, 8)
    vu_load = load(value_up.at[0], vu, 9)
    op_load = load(output_proj.at[0], op, 10)

    hid_load.wait()
    rows = hid[...]
    qd_load.wait()
    wide = jnp.dot(rows, qd[...], preferred_element_type=F32)
    for t in range(QT):
        part_q[t // 3, t % 3] = wide[:, t * 128 : (t + 1) * 128]

    pl.semaphore_wait(barrier, NZ + NY)

    for dy in (2, 1, 3):
        chunk = part_q.at[lax.rem(y + dy, NY)]
        send(chunk, y_q.at[NY - 1 - dy], 0, recv_sem.at[0], at(0, dy))
    ld_load.wait()
    wide = jnp.dot(rows, ld[...], preferred_element_type=F32)
    empty = jnp.zeros((SEQ, 128 - ROPE), F32)
    rope = jnp.concatenate([wide[:, LAT:], empty], axis=1)
    for t in range(KT):
        part_k[t, 0] = wide[:, t * 128 : (t + 1) * 128]
        part_k[t, 1] = rope
    for dy in (2, 1, 3):
        chunk = part_k.at[lax.rem(y + dy, NY)]
        send(chunk, y_k.at[NY - 1 - dy], 1, recv_sem.at[1], at(0, dy))
    own_rows = rows.astype(F32)
    right_rows = jnp.concatenate([own_rows[:, 128:], jnp.zeros((SEQ, 32), F32)], axis=1)
    x_out[...] = jnp.concatenate([own_rows[:, :128], right_rows], axis=0).astype(BF16)
    send(x_out, x_in, 2, recv_sem.at[2], {"section": after})

    wait_bytes(y_q, recv_sem.at[0])
    own_qs[...] = part_q[y] + y_q[0] + y_q[1] + y_q[2]
    for dz in (4, 3, 5, 2, 6, 1, 7):
        send(own_qs, z_q.at[NZ - 1 - dz], 3, recv_sem.at[3], at(dz, 0))
    wait_bytes(y_k, recv_sem.at[1])
    own_ks[...] = part_k[y] + y_k[0] + y_k[1] + y_k[2]
    for dz in (4, 3, 5, 2, 6, 1, 7):
        send(own_ks, z_k.at[NZ - 1 - dz], 4, recv_sem.at[4], at(dz, 0))

    wait_bytes(z_q, recv_sem.at[3])
    lat_q[y] = functools.reduce(jnp.add, [own_qs[...]] + [z_q[k] for k in range(NZ - 1)])
    for dy in (2, 1, 3):
        send(lat_q.at[y], lat_q.at[y], 5, recv_sem.at[5], at(0, dy))
    pl.semaphore_signal(next_sem, inc=1, device_id={"section": before}, device_id_type=MESH)
    wait_bytes(z_k, recv_sem.at[4])
    sums = functools.reduce(jnp.add, [own_ks[...]] + [z_k[k] for k in range(NZ - 1)])
    lat_k[y] = sums[0]
    new_rope = sums[1]
    for dy in (2, 1, 3):
        send(lat_k.at[y], lat_k.at[y], 6, recv_sem.at[6], at(0, dy))
    qgain_load.wait()
    qu_load.wait()
    wait_bytes(lat_q.at[pl.ds(0, NY - 1)], recv_sem.at[5])

    tiles = [lat_q[t // 3, t % 3] for t in range(QT)]
    squares = functools.reduce(jnp.add, [tile * tile for tile in tiles])
    mean = jnp.sum(squares, axis=1, keepdims=True) * (1.0 / QL)
    q_scale = lax.rsqrt(mean + 1e-06)
    query_norm = jnp.concatenate(
        [tiles[t] * q_scale * qgain[0:1, t * 128 : (t + 1) * 128] for t in range(QT)], axis=1
    ).astype(BF16)
    own = jnp.dot(query_norm, qu[...], preferred_element_type=F32)
    first = own[:, :PADKW]
    second = pltpu.roll(own[:, LAT:], PADKW - ROPE, axis=1)
    own_q = jnp.concatenate([first, second], axis=0).astype(BF16)
    q_all[0] = own_q[:, :LAT]
    q_rope[0, 0] = own_q[:, LAT:]

    for dz in (4, 3, 5, 2, 6, 1, 7):
        slot = (NZ - dz) * NY
        send(q_all.at[0], q_all.at[slot], 7, qz_sem.at[NZ - dz], at(dz, 0))
    for dy in (2, 1, 3):
        send(q_rope.at[0, 0], q_rope.at[0, NY - dy], 8, rope_sem.at[2], at(0, dy))
    for dy in (2, 1, 3):
        send(q_all.at[0], q_all.at[NY - dy], 9, qy_sem.at[0], at(0, dy))

    wait_bytes(lat_k.at[pl.ds(0, NY - 1)], recv_sem.at[6])
    lgain_load.wait()
    tiles = [lat_k[t] for t in range(KT)]
    squares = functools.reduce(jnp.add, [tile * tile for tile in tiles])
    mean = jnp.sum(squares, axis=1, keepdims=True) * (1.0 / LAT)
    kv_scale = lax.rsqrt(mean + 1e-06)
    new_key = jnp.concatenate(
        [tiles[t] * kv_scale * lgain[0:1, t * 128 : (t + 1) * 128] for t in range(KT)]
        + [new_rope],
        axis=1,
    )
    new_key = new_key.astype(BF16).astype(F32)
    new_key = jnp.concatenate([new_key, new_key], axis=0)
    new_score = jnp.sum(own_q.astype(F32) * new_key, axis=1, keepdims=True) * SCALE

    chosen_load.wait()
    picked = chosen[...]
    lane = lax.broadcasted_iota(jnp.int32, (SEQ, POS), 1)
    hits = jnp.zeros((SEQ, POS), F32)
    for j in range(POS // BLK):
        hit = jnp.where(picked == me * (POS // BLK) + j, 1.0, 0.0)
        hit = jnp.max(hit, axis=1, keepdims=True)
        hits = jnp.where(lane // BLK == j, hit, hits)
    position = lax.broadcasted_iota(jnp.int32, (1, POS), 1) + me * POS
    limits_load.wait()

    def forward(r):
        block = q_all.at[r * NY]
        wait_bytes(block, qz_sem.at[r])
        for dy in (2, 1, 3):
            target = q_all.at[r * NY + NY - dy]
            send(block, target, 9, qy_sem.at[GROUP_OF[r]], at(0, dy))

    forward(1)
    forward(7)
    wait_bytes(q_rope.at[0, pl.ds(0, NY - 1)], rope_sem.at[2])
    for dz in (4, 3, 5, 2, 6, 1, 7):
        r = NZ - dz
        send(q_rope.at[0], q_rope.at[r], 10, rope_sem.at[GROUP_OF[r]], at(dz, 0))
    for r in ORDER[3:]:
        forward(r)

    kv_load.wait()
    row = lax.broadcasted_iota(jnp.int32, (HALF // SEQ, 1), 0)
    places = row // (2 * NY) * 6

    def attend(g):
        wait_bytes(q_all.at[pl.ds(0, 4 * (NY - 1))], qy_sem.at[g])
        wait_bytes(q_rope.at[pl.ds(0, 3 + g)], rope_sem.at[g])
        base = g * HALF
        for p, r in enumerate(GROUPS[g]):
            for k in range(NY):
                rows_at = base + (p * NY + k) * 16
                block = q_all[r * NY + k].astype(F32)
                for t in range(KT):
                    q_f32[t, rows_at : rows_at + 16, :] = block[:, t * 128 : (t + 1) * 128]
                q_f32[KT, rows_at : rows_at + 16, :] = q_rope[r, k].astype(F32)
        for b in range(SEQ):
            queries = jnp.concatenate(
                [q_f32[t, pl.ds(base + b, HALF // SEQ, stride=SEQ), :] for t in range(KT + 1)],
                axis=1,
            )
            queries = queries[:, :KW].astype(BF16)
            keys = kv[b]
            scores = jnp.dot(queries, keys, preferred_element_type=F32) * SCALE
            valid = (hits[b : b + 1, :] > 0.5) & (position < limits[0, b])
            masked = jnp.where(valid, scores, -1e30)
            top = jnp.max(masked, axis=1, keepdims=True)
            expo = jnp.where(valid, jnp.exp(masked - top), 0.0)
            total = jnp.sum(expo, axis=1, keepdims=True)
            summed = folded(
                lax.dot_general(
                    two_rows(expo),
                    keys[:LAT],
                    (((1,), (1,)), ((), ())),
                    preferred_element_type=F32,
                )
            )
            rows_at = pl.ds(base + b, HALF // SEQ, stride=SEQ)
            for t in range(KT):
                o_f32[t, rows_at, :] = summed[:, t * 128 : (t + 1) * 128]
            s_f32[rows_at, :] = stats_tile(top, total, places)

    def rows_of(g, p, k):
        start = g * HALF + (p * NY + k) * 16
        return slice(start, start + 16)

    def sums_of(g, p, k):
        return jnp.concatenate([o_f32[t, rows_of(g, p, k), :] for t in range(KT)], axis=1)

    def send_sums(g):
        for k in (2, 1, 3):
            stats = [s_f32[rows_of(g, p, k), :] for p in range(4)]
            s_out[g, k] = functools.reduce(jnp.add, stats).astype(BF16)
            send(s_out.at[g, k], ys_in.at[g, NY - 1 - k], 11, ds_sem.at[g], at(0, k))
        for r in SEND_ORDER[g]:
            p = GROUPS[g].index(r)
            for k in (2, 1, 3):
                o_out[r, k] = sums_of(g, p, k).astype(BF16)
                send(o_out.at[r, k], y_in.at[r, NY - 1 - k], 12, dy_sem.at[r], at(0, k))

    def join_sums(g):
        wait_bytes(ys_in.at[g], ds_sem.at[g])
        for r in SEND_ORDER[g]:
            p = GROUPS[g].index(r)
            wait_bytes(y_in.at[r], dy_sem.at[r])
            parts = [(sums_of(g, p, 0), *read_stats(s_f32[rows_of(g, p, 0), :], 6 * p))]
            for k in range(NY - 1):
                stats = read_stats(ys_in[g, k].astype(F32), 6 * p)
                parts.append((y_in[r, k].astype(F32), *stats))
            summed, top, total = merged(parts)
            if r == 0:
                return summed, top, total
            wide = jnp.concatenate([summed, stats_tile(top, total)], axis=1)
            c_out[r - 1] = wide.astype(BF16)
            send(c_out.at[r - 1], z_in.at[NZ - 1 - r], 13, recv_sem.at[7], at(r, 0))

    attend(0)
    send_sums(0)
    attend(1)
    send_sums(1)
    own_part = join_sums(0)
    join_sums(1)
    wait_bytes(z_in, recv_sem.at[7])
    parts = [own_part, (new_key[:, :LAT], new_score, jnp.ones((2 * SEQ, 1), F32))]
    for k in range(NZ - 1):
        block = z_in[k].astype(F32)
        parts.append((block[:, :LAT], *read_stats(block[:, LAT:])))
    summed, _, total = merged(parts)
    attended = summed / total

    vu_load.wait()
    heads = []
    for h in range(2):
        both = two_rows(attended[h * SEQ : (h + 1) * SEQ, :])
        heads.append(folded(jnp.dot(both, vu[h], preferred_element_type=F32)))
    head_out = two_rows(jnp.concatenate(heads, axis=1))
    op_load.wait()
    pl.semaphore_wait(next_sem, 1)
    width = NY * FEAT
    for r in FAR_FIRST:
        zt = lax.rem(z + r, NZ)
        columns = op[:, pl.ds(pl.multiple_of(zt * width, 128), width)]
        projected = folded(jnp.dot(head_out, columns, preferred_element_type=F32))
        for k in range(NY):
            start = k * FEAT // 128 * 128
            shift = k * FEAT - start
            stop = -(-(k * FEAT + FEAT) // 128) * 128
            piece = projected[:, start:stop]
            if shift:
                piece = pltpu.roll(piece, stop - start - shift, axis=1)
            block = jnp.concatenate([piece[:, :128], piece[:, 128:256]], axis=0)
            e_out[r * NY + k] = block.astype(BF16)
            slot = (NZ - r) % NZ * NY + y
            target = {"section": after, "cache": zt * NY + k}
            send(e_out.at[r * NY + k], e_in.at[slot], 14, recv_sem.at[8], target)

    wait_bytes(x_in, recv_sem.at[2])
    total = x_in[...].astype(F32)
    wait_bytes(e_in, recv_sem.at[8])
    for slot in range(NC):
        total = total + e_in[slot].astype(F32)
    out[0, :, :128] = total[:SEQ]
    out[0, :, 128:] = total[SEQ:, : FEAT - 128]

    wait_bytes(y_q, send_sem.at[0])
    wait_bytes(y_k, send_sem.at[1])
    wait_bytes(x_out, send_sem.at[2])
    wait_bytes(z_q, send_sem.at[3])
    wait_bytes(z_k, send_sem.at[4])
    wait_bytes(lat_q.at[pl.ds(0, NY - 1)], send_sem.at[5])
    wait_bytes(lat_k.at[pl.ds(0, NY - 1)], send_sem.at[6])
    wait_bytes(q_all.at[pl.ds(0, NZ - 1)], send_sem.at[7])
    wait_bytes(q_rope.at[0, pl.ds(0, NY - 1)], send_sem.at[8])
    wait_bytes(q_all.at[pl.ds(0, NC - NZ)], send_sem.at[9])
    wait_bytes(q_rope.at[pl.ds(0, NZ - 1)], send_sem.at[10])
    wait_bytes(ys_in, send_sem.at[11])
    wait_bytes(y_in, send_sem.at[12])
    wait_bytes(z_in, send_sem.at[13])
    wait_bytes(e_out, send_sem.at[14])


def on_device(*arrays):
    arrays = list(arrays)
    arrays[8] = jnp.swapaxes(arrays[8], 2, 3)
    vmem = pl.BlockSpec(memory_space=pltpu.VMEM)
    hbm = pl.BlockSpec(memory_space=pl.ANY)
    dma = pltpu.SemaphoreType.DMA
    return pl.pallas_call(
        kernel,
        out_shape=pltpu.VMEM((1, SEQ, FEAT), F32),
        in_specs=[hbm] * 11,
        out_specs=vmem,
        scratch_shapes=[
            pltpu.VMEM((SEQ, FEAT), BF16),
            pltpu.VMEM((1, QL), F32),
            pltpu.VMEM((1, LAT), F32),
            pltpu.VMEM((SEQ, 32), jnp.int32),
            pltpu.SMEM((1, SEQ), jnp.int32),
            pltpu.VMEM((FEAT, QL), BF16),
            pltpu.VMEM((FEAT, KW), BF16),
            pltpu.VMEM((QL, 2 * KW), BF16),
            pltpu.VMEM((2, LAT, HV), BF16),
            pltpu.VMEM((2 * HV, NC * FEAT), BF16),
            pltpu.VMEM((SEQ, KW, POS), BF16),
            pltpu.VMEM((NY, 3, SEQ, 128), F32),
            pltpu.VMEM((NY, 2, SEQ, 128), F32),
            pltpu.VMEM((NY - 1, 3, SEQ, 128), F32),
            pltpu.VMEM((NY - 1, 2, SEQ, 128), F32),
            pltpu.VMEM((3, SEQ, 128), F32),
            pltpu.VMEM((2, SEQ, 128), F32),
            pltpu.VMEM((NZ - 1, 3, SEQ, 128), F32),
            pltpu.VMEM((NZ - 1, 2, SEQ, 128), F32),
            pltpu.VMEM((NY, 3, SEQ, 128), F32),
            pltpu.VMEM((NY, SEQ, 128), F32),
            pltpu.VMEM((NC, 16, LAT), BF16),
            pltpu.VMEM((NZ, NY, 16, 128), BF16),
            pltpu.VMEM((KT + 1, NC * 16, 128), F32),
            pltpu.VMEM((KT, NC * 16, 128), F32),
            pltpu.VMEM((NC * 16, 128), F32),
            pltpu.VMEM((NZ, NY, 16, LAT), BF16),
            pltpu.VMEM((2, NY, 16, 128), BF16),
            pltpu.VMEM((NZ, NY - 1, 16, LAT), BF16),
            pltpu.VMEM((2, NY - 1, 16, 128), BF16),
            pltpu.VMEM((NZ - 1, 16, PADKW), BF16),
            pltpu.VMEM((NZ - 1, 16, PADKW), BF16),
            pltpu.VMEM((NC, 16, 128), BF16),
            pltpu.VMEM((NC, 16, 128), BF16),
            pltpu.VMEM((16, 128), BF16),
            pltpu.VMEM((16, 128), BF16),
            dma((11,)),
            dma((15,)),
            dma((9,)),
            dma((NZ,)),
            dma((2,)),
            dma((3,)),
            dma((NZ,)),
            dma((2,)),
            pltpu.SemaphoreType.REGULAR,
        ],
        compiler_params=pltpu.CompilerParams(
            collective_id=0, has_side_effects=True, vmem_limit_bytes=60 << 20
        ),
        cost_estimate=pl.CostEstimate(
            flops=400_000_000, bytes_accessed=11_000_000, transcendentals=200_000
        ),
    )(*arrays)


def solution(mesh):
    return jax.shard_map(
        on_device,
        mesh=mesh,
        in_specs=(
            P("section", None, "cache"),
            P("section", "cache", None),
            P("section", "cache", None),
            P("section", None),
            P("section", None),
            P("section", None, "cache"),
            P("section", "cache", None, None),
            P("section", "cache", None),
            P("section", None, "cache", None),
            P("section", None, None),
            P("section", None),
        ),
        out_specs=P("section", None, "cache"),
        check_vma=False,
    )
```

```python
import functools

import jax
import jax.numpy as jnp
from jax import lax
from jax.experimental import pallas as pl
from jax.experimental.pallas import tpu as pltpu
from jax.sharding import PartitionSpec as P

MESH = pl.DeviceIdType.MESH
F32 = jnp.float32
BF16 = jnp.bfloat16

SEQ = 8
QL = 1536
LAT = 512
ROPE = 64
HV = 128
BLK = 64
KW = 576
PADKW = 640
NZ = 8
NY = 4
NC = NZ * NY
NSEC = 8
FEAT = 224
POS = 256
QT = QL // 128
KT = LAT // 128
SCALE = (HV + ROPE) ** (-0.5)
GROUPS = ((0, 1, 7, 2, 6, 3, 5, 4),)
DIRECT_Q = (1, 7, 2, 6)
DIRECT_SUM = (2, 6, 1, 7)
SUM_ORDER = ((4, 3, 5, 0),)
ORDER = sum(GROUPS, ())
STARTS = tuple(sum(len(group) for group in GROUPS[:g]) * NY * 16 for g in range(len(GROUPS)))
FAR_FIRST = (4, 3, 5, 2, 6, 1, 7, 0)


def split_three(value):
    high = value.astype(BF16).astype(F32)
    rest = value - high
    middle = rest.astype(BF16).astype(F32)
    return high, middle, rest - middle


def two_rows(value):
    high = value.astype(BF16)
    low = (value - high.astype(F32)).astype(BF16)
    return jnp.concatenate([high.astype(F32), low.astype(F32)], axis=0).astype(BF16)


def folded(value):
    half = value.shape[0] // 2
    return value[:half] + value[half:]


def stats_tile(top, total, places=0):
    lane = lax.broadcasted_iota(jnp.int32, (top.shape[0], 128), 1) - places
    stats = jnp.zeros((top.shape[0], 128), F32)
    for at, piece in enumerate(split_three(top) + split_three(total)):
        stats = jnp.where(lane == at, piece, stats)
    return stats


def read_stats(stats, place=0):
    lane = lax.broadcasted_iota(jnp.int32, stats.shape, 1) - place
    top = jnp.where((lane >= 0) & (lane < 3), stats, 0.0)
    total = jnp.where((lane >= 3) & (lane < 6), stats, 0.0)
    return jnp.sum(top, axis=1, keepdims=True), jnp.sum(total, axis=1, keepdims=True)


def merged(parts):
    top = functools.reduce(jnp.maximum, [p[1] for p in parts])
    scales = [jnp.exp(p[1] - top) for p in parts]
    total = functools.reduce(jnp.add, [p[2] * a for p, a in zip(parts, scales)])
    summed = functools.reduce(jnp.add, [p[0] * a for p, a in zip(parts, scales)])
    return summed, top, total


def kernel(
    hidden,
    query_down,
    latent_down,
    query_gain,
    latent_gain,
    query_up,
    value_up,
    output_proj,
    latent_cache,
    selected,
    lengths,
    out,
    hid,
    qgain,
    lgain,
    chosen,
    limits,
    qd,
    ld,
    qu,
    vu,
    op,
    kv,
    part_q,
    part_k,
    y_q,
    y_k,
    own_qs,
    own_ks,
    z_q,
    z_k,
    lat_q,
    lat_k,
    q_all,
    q_rope,
    r_in,
    q_f32,
    o_f32,
    s_f32,
    o_out,
    s_out,
    y_in,
    ys_in,
    c_out,
    z_in,
    f_out,
    f_in,
    e_out,
    e_in,
    x_out,
    x_in,
    load_sem,
    send_sem,
    recv_sem,
    qz_sem,
    qy_sem,
    rope_sem,
    dy_sem,
    ds_sem,
    next_sem,
):
    sec = lax.axis_index("section")
    me = lax.axis_index("cache")
    z = me // NY
    y = me % NY
    after = lax.rem(sec + 1, NSEC)
    before = lax.rem(sec + NSEC - 1, NSEC)

    def at(dz, dy):
        return {"cache": lax.rem(z + dz, NZ) * NY + lax.rem(y + dy, NY)}

    def load(source, target, index):
        copy = pltpu.make_async_copy(source, target, load_sem.at[index])
        copy.start()
        return copy

    def send(source, target, send_index, recv, device):
        pltpu.make_async_remote_copy(
            src_ref=source,
            dst_ref=target,
            send_sem=send_sem.at[send_index],
            recv_sem=recv,
            device_id=device,
            device_id_type=MESH,
        ).start()

    def wait_bytes(ref, sem):
        pltpu.make_async_copy(ref, ref, sem).wait()

    barrier = pltpu.get_barrier_semaphore()
    for dz in (4, 3, 5, 2, 6, 1, 7):
        pl.semaphore_signal(barrier, inc=1, device_id=at(dz, 0), device_id_type=MESH)
    for dy in (2, 1, 3):
        pl.semaphore_signal(barrier, inc=1, device_id=at(0, dy), device_id_type=MESH)
    for other in (after, before):
        pl.semaphore_signal(barrier, inc=1, device_id={"section": other}, device_id_type=MESH)

    hid_load = load(hidden.at[0], hid, 0)
    qd_load = load(query_down.at[0], qd, 1)
    ld_load = load(latent_down.at[0], ld, 2)
    qgain_load = load(query_gain, qgain, 3)
    lgain_load = load(latent_gain, lgain, 4)
    chosen_load = load(selected.at[0], chosen, 5)
    limits_load = load(lengths, limits, 6)
    qu_load = load(query_up.at[0], qu, 7)
    kv_load = load(latent_cache.at[0], kv, 8)
    vu_load = load(value_up.at[0], vu, 9)
    op_load = load(output_proj.at[0], op, 10)

    hid_load.wait()
    rows = hid[...]
    qd_load.wait()
    wide = jnp.dot(rows, qd[...], preferred_element_type=F32)
    for t in range(QT):
        part_q[t // 3, t % 3] = wide[:, t * 128 : (t + 1) * 128]

    pl.semaphore_wait(barrier, NZ + NY)

    for dy in (2, 1, 3):
        chunk = part_q.at[lax.rem(y + dy, NY)]
        send(chunk, y_q.at[NY - 1 - dy], 0, recv_sem.at[0], at(0, dy))
    ld_load.wait()
    wide = jnp.dot(rows, ld[...], preferred_element_type=F32)
    empty = jnp.zeros((SEQ, 128 - ROPE), F32)
    rope = jnp.concatenate([wide[:, LAT:], empty], axis=1)
    for t in range(KT):
        part_k[t, 0] = wide[:, t * 128 : (t + 1) * 128]
        part_k[t, 1] = rope
    for dy in (2, 1, 3):
        chunk = part_k.at[lax.rem(y + dy, NY)]
        send(chunk, y_k.at[NY - 1 - dy], 1, recv_sem.at[1], at(0, dy))
    own_rows = rows.astype(F32)
    right_rows = jnp.concatenate([own_rows[:, 128:], jnp.zeros((SEQ, 32), F32)], axis=1)
    x_out[...] = jnp.concatenate([own_rows[:, :128], right_rows], axis=0).astype(BF16)
    send(x_out, x_in, 2, recv_sem.at[2], {"section": after})

    wait_bytes(y_q, recv_sem.at[0])
    own_qs[...] = part_q[y] + y_q[0] + y_q[1] + y_q[2]
    for dz in (4, 3, 5, 2, 6, 1, 7):
        send(own_qs, z_q.at[NZ - 1 - dz], 3, recv_sem.at[3], at(dz, 0))
    wait_bytes(y_k, recv_sem.at[1])
    own_ks[...] = part_k[y] + y_k[0] + y_k[1] + y_k[2]
    for dz in (4, 3, 5, 2, 6, 1, 7):
        send(own_ks, z_k.at[NZ - 1 - dz], 4, recv_sem.at[4], at(dz, 0))

    wait_bytes(z_q, recv_sem.at[3])
    lat_q[y] = functools.reduce(jnp.add, [own_qs[...]] + [z_q[k] for k in range(NZ - 1)])
    for dy in (2, 1, 3):
        send(lat_q.at[y], lat_q.at[y], 5, recv_sem.at[5], at(0, dy))
    pl.semaphore_signal(next_sem, inc=1, device_id={"section": before}, device_id_type=MESH)
    wait_bytes(z_k, recv_sem.at[4])
    sums = functools.reduce(jnp.add, [own_ks[...]] + [z_k[k] for k in range(NZ - 1)])
    lat_k[y] = sums[0]
    new_rope = sums[1]
    for dy in (2, 1, 3):
        send(lat_k.at[y], lat_k.at[y], 6, recv_sem.at[6], at(0, dy))
    qgain_load.wait()
    qu_load.wait()
    wait_bytes(lat_q.at[pl.ds(0, NY - 1)], recv_sem.at[5])

    tiles = [lat_q[t // 3, t % 3] for t in range(QT)]
    squares = functools.reduce(jnp.add, [tile * tile for tile in tiles])
    mean = jnp.sum(squares, axis=1, keepdims=True) * (1.0 / QL)
    q_scale = lax.rsqrt(mean + 1e-06)
    query_norm = jnp.concatenate(
        [tiles[t] * q_scale * qgain[0:1, t * 128 : (t + 1) * 128] for t in range(QT)], axis=1
    ).astype(BF16)
    own = jnp.dot(query_norm, qu[...], preferred_element_type=F32)
    first = own[:, :PADKW]
    second = pltpu.roll(own[:, LAT:], PADKW - ROPE, axis=1)
    own_q = jnp.concatenate([first, second], axis=0).astype(BF16)
    q_all[0] = own_q[:, :LAT]
    lane = lax.broadcasted_iota(jnp.int32, (SEQ, 128), 1)
    pair = jnp.where(lane < ROPE, own[:, LAT : LAT + 128], own[:, 2 * KW - 128 :])
    r_in[0] = jnp.concatenate([pair, jnp.zeros((SEQ, 128), F32)], axis=0).astype(BF16)

    for dz in (4, 3, 5, 2, 6, 1, 7):
        r = NZ - dz
        if r in DIRECT_Q:
            for dy in (2, 1, 3, 0):
                target = q_all.at[r * NY + (NY - dy) % NY]
                send(q_all.at[0], target, 7, qy_sem.at[r], at(dz, dy))
        else:
            send(q_all.at[0], q_all.at[r * NY], 7, qz_sem.at[r], at(dz, 0))
    for dy in (2, 1, 3):
        send(r_in.at[0], r_in.at[NY - dy], 8, rope_sem.at[0], at(0, dy))
    for dy in (2, 1, 3):
        send(q_all.at[0], q_all.at[NY - dy], 9, qy_sem.at[0], at(0, dy))

    wait_bytes(lat_k.at[pl.ds(0, NY - 1)], recv_sem.at[6])
    lgain_load.wait()
    tiles = [lat_k[t] for t in range(KT)]
    squares = functools.reduce(jnp.add, [tile * tile for tile in tiles])
    mean = jnp.sum(squares, axis=1, keepdims=True) * (1.0 / LAT)
    kv_scale = lax.rsqrt(mean + 1e-06)
    new_key = jnp.concatenate(
        [tiles[t] * kv_scale * lgain[0:1, t * 128 : (t + 1) * 128] for t in range(KT)]
        + [new_rope],
        axis=1,
    )
    new_key = new_key.astype(BF16).astype(F32)
    new_key = jnp.concatenate([new_key, new_key], axis=0)
    new_score = jnp.sum(own_q.astype(F32) * new_key, axis=1, keepdims=True) * SCALE

    chosen_load.wait()
    picked = chosen[...]
    lane = lax.broadcasted_iota(jnp.int32, (SEQ, POS), 1)
    hits = jnp.zeros((SEQ, POS), F32)
    for j in range(POS // BLK):
        hit = jnp.where(picked == me * (POS // BLK) + j, 1.0, 0.0)
        hit = jnp.max(hit, axis=1, keepdims=True)
        hits = jnp.where(lane // BLK == j, hit, hits)
    position = lax.broadcasted_iota(jnp.int32, (1, POS), 1) + me * POS
    limits_load.wait()

    def forward(r):
        block = q_all.at[r * NY]
        wait_bytes(block, qz_sem.at[r])
        for dy in (2, 1, 3):
            target = q_all.at[r * NY + NY - dy]
            send(block, target, 9, qy_sem.at[r], at(0, dy))

    wait_bytes(r_in.at[pl.ds(0, NY - 1)], rope_sem.at[0])
    for k in range(2):
        two = [r_in[2 * k].astype(F32)[:SEQ], r_in[2 * k + 1].astype(F32)[:SEQ]]
        q_rope[0, k] = jnp.concatenate(two, axis=0).astype(BF16)
    for dz in (4, 3, 5, 2, 6, 1, 7):
        r = NZ - dz
        send(q_rope.at[0], q_rope.at[r], 10, rope_sem.at[r], at(dz, 0))
    for r in (1, 7, 2, 6, 3, 5, 4):
        if r not in DIRECT_Q:
            forward(r)

    kv_load.wait()

    def attend(g):
        base = STARTS[g]
        heads = len(GROUPS[g]) * NY * 2
        row = lax.broadcasted_iota(jnp.int32, (heads, 1), 0)
        places = row // (2 * NY) * 6
        for p, r in enumerate(GROUPS[g]):
            arriving = NY if r in DIRECT_Q else NY - 1
            wait_bytes(q_all.at[pl.ds(0, arriving)], qy_sem.at[r])
            if r > 0:
                wait_bytes(q_rope.at[r], rope_sem.at[r])
            for k in range(NY):
                rows_at = base + (p * NY + k) * 16
                block = q_all[r * NY + k].astype(F32)
                for t in range(KT):
                    q_f32[t, rows_at : rows_at + 16, :] = block[:, t * 128 : (t + 1) * 128]
            for k in range(2):
                two = q_rope[r, k].astype(F32)
                other = pltpu.roll(two, ROPE, axis=1)
                for m in range(2):
                    rows_at = base + (p * NY + 2 * k + m) * 16
                    own_rows = slice(m * SEQ, (m + 1) * SEQ)
                    q_f32[KT, rows_at : rows_at + SEQ, :] = two[own_rows]
                    q_f32[KT, rows_at + SEQ : rows_at + 16, :] = other[own_rows]
        for b in range(SEQ):
            queries = jnp.concatenate(
                [q_f32[t, pl.ds(base + b, heads, stride=SEQ), :] for t in range(KT + 1)],
                axis=1,
            )
            queries = queries[:, :KW].astype(BF16)
            keys = kv[b]
            scores = jnp.dot(queries, keys, preferred_element_type=F32) * SCALE
            valid = (hits[b : b + 1, :] > 0.5) & (position < limits[0, b])
            masked = jnp.where(valid, scores, -1e30)
            top = jnp.max(masked, axis=1, keepdims=True)
            expo = jnp.where(valid, jnp.exp(masked - top), 0.0)
            total = jnp.sum(expo, axis=1, keepdims=True)
            summed = folded(
                lax.dot_general(
                    two_rows(expo),
                    keys[:LAT],
                    (((1,), (1,)), ((), ())),
                    preferred_element_type=F32,
                )
            )
            rows_at = pl.ds(base + b, heads, stride=SEQ)
            for t in range(KT):
                o_f32[t, rows_at, :] = summed[:, t * 128 : (t + 1) * 128]
            s_f32[rows_at, :] = stats_tile(top, total, places)

    def rows_of(g, p, k):
        start = STARTS[g] + (p * NY + k) * 16
        return slice(start, start + 16)

    def sums_of(g, p, k):
        return jnp.concatenate([o_f32[t, rows_of(g, p, k), :] for t in range(KT)], axis=1)

    def send_sums(g):
        staged = [GROUPS[g].index(r) for r in SUM_ORDER[g]]
        for k in (2, 1, 3):
            stats = [s_f32[rows_of(g, p, k), :] for p in staged]
            s_out[g, k] = functools.reduce(jnp.add, stats).astype(BF16)
            send(s_out.at[g, k], ys_in.at[g, NY - 1 - k], 11, ds_sem.at[g], at(0, k))
        for r in SUM_ORDER[g]:
            p = GROUPS[g].index(r)
            for k in (2, 1, 3):
                o_out[r, k] = sums_of(g, p, k).astype(BF16)
                send(o_out.at[r, k], y_in.at[r, NY - 1 - k], 12, dy_sem.at[r], at(0, k))
        for f, r in enumerate(DIRECT_SUM):
            if r in GROUPS[g]:
                p = GROUPS[g].index(r)
                to = DIRECT_SUM.index(NZ - r) * NY
                for k in (2, 1, 3, 0):
                    stats = s_f32[rows_of(g, p, k), :]
                    stats = pltpu.roll(stats, (128 - 6 * p) % 128, axis=1) if p else stats
                    wide = jnp.concatenate([sums_of(g, p, k), stats], axis=1)
                    f_out[f * NY + k] = wide.astype(BF16)
                    target = f_in.at[to + (NY - k) % NY]
                    send(f_out.at[f * NY + k], target, 15, recv_sem.at[9], at(r, k))

    def join_sums(g):
        wait_bytes(ys_in.at[g], ds_sem.at[g])
        for r in SUM_ORDER[g]:
            p = GROUPS[g].index(r)
            wait_bytes(y_in.at[r], dy_sem.at[r])
            parts = [(sums_of(g, p, 0), *read_stats(s_f32[rows_of(g, p, 0), :], 6 * p))]
            for k in range(NY - 1):
                stats = read_stats(ys_in[g, k].astype(F32), 6 * p)
                parts.append((y_in[r, k].astype(F32), *stats))
            summed, top, total = merged(parts)
            if r == 0:
                return summed, top, total
            wide = jnp.concatenate([summed, stats_tile(top, total)], axis=1)
            c_out[r] = wide.astype(BF16)
            send(c_out.at[r], z_in.at[NZ - r], 13, recv_sem.at[7], at(r, 0))

    for g in range(len(GROUPS)):
        attend(g)
        send_sums(g)
    own_parts = [join_sums(g) for g in range(len(GROUPS))]
    parts = [part for part in own_parts if part is not None]
    parts.append((new_key[:, :LAT], new_score, jnp.ones((2 * SEQ, 1), F32)))

    def joined_with(parts, blocks):
        for block in blocks:
            block = block.astype(F32)
            parts = parts + [(block[:, :LAT], *read_stats(block[:, LAT:]))]
        return merged(parts)

    if DIRECT_SUM:
        wait_bytes(f_in, recv_sem.at[9])
        parts = [joined_with(parts, [f_in[k] for k in range(len(DIRECT_SUM) * NY)])]
    staged = sum(SUM_ORDER, ())
    wait_bytes(z_in.at[pl.ds(0, len(staged) - 1)], recv_sem.at[7])
    summed, _, total = joined_with(parts, [z_in[r] for r in range(1, NZ) if r in staged])
    attended = summed / total

    vu_load.wait()
    heads = []
    for h in range(2):
        both = two_rows(attended[h * SEQ : (h + 1) * SEQ, :])
        heads.append(folded(jnp.dot(both, vu[h], preferred_element_type=F32)))
    head_out = two_rows(jnp.concatenate(heads, axis=1))
    op_load.wait()
    pl.semaphore_wait(next_sem, 1)
    width = NY * FEAT
    for r in FAR_FIRST:
        zt = lax.rem(z + r, NZ)
        columns = op[:, pl.ds(pl.multiple_of(zt * width, 128), width)]
        projected = folded(jnp.dot(head_out, columns, preferred_element_type=F32))
        for k in range(NY):
            start = k * FEAT // 128 * 128
            shift = k * FEAT - start
            stop = -(-(k * FEAT + FEAT) // 128) * 128
            piece = projected[:, start:stop]
            if shift:
                piece = pltpu.roll(piece, stop - start - shift, axis=1)
            block = jnp.concatenate([piece[:, :128], piece[:, 128:256]], axis=0)
            e_out[r * NY + k] = block.astype(BF16)
            slot = (NZ - r) % NZ * NY + y
            target = {"section": after, "cache": zt * NY + k}
            send(e_out.at[r * NY + k], e_in.at[slot], 14, recv_sem.at[8], target)

    wait_bytes(x_in, recv_sem.at[2])
    total = x_in[...].astype(F32)
    wait_bytes(e_in, recv_sem.at[8])
    for slot in range(NC):
        total = total + e_in[slot].astype(F32)
    out[0, :, :128] = total[:SEQ]
    out[0, :, 128:] = total[SEQ:, : FEAT - 128]

    wait_bytes(y_q, send_sem.at[0])
    wait_bytes(y_k, send_sem.at[1])
    wait_bytes(x_out, send_sem.at[2])
    wait_bytes(z_q, send_sem.at[3])
    wait_bytes(z_k, send_sem.at[4])
    wait_bytes(lat_q.at[pl.ds(0, NY - 1)], send_sem.at[5])
    wait_bytes(lat_k.at[pl.ds(0, NY - 1)], send_sem.at[6])
    straight = len(DIRECT_Q)
    wait_bytes(q_all.at[pl.ds(0, NZ - 1 + (NY - 1) * straight)], send_sem.at[7])
    wait_bytes(r_in.at[pl.ds(0, NY - 1)], send_sem.at[8])
    wait_bytes(q_all.at[pl.ds(0, (NZ - straight) * (NY - 1))], send_sem.at[9])
    wait_bytes(q_rope.at[pl.ds(0, NZ - 1)], send_sem.at[10])
    wait_bytes(ys_in, send_sem.at[11])
    wait_bytes(y_in.at[pl.ds(0, len(staged))], send_sem.at[12])
    wait_bytes(z_in.at[pl.ds(0, len(staged) - 1)], send_sem.at[13])
    if DIRECT_SUM:
        wait_bytes(f_out, send_sem.at[15])
    wait_bytes(e_out, send_sem.at[14])


def on_device(*arrays):
    arrays = list(arrays)
    arrays[8] = jnp.swapaxes(arrays[8], 2, 3)
    vmem = pl.BlockSpec(memory_space=pltpu.VMEM)
    hbm = pl.BlockSpec(memory_space=pl.ANY)
    dma = pltpu.SemaphoreType.DMA
    return pl.pallas_call(
        kernel,
        out_shape=pltpu.VMEM((1, SEQ, FEAT), F32),
        in_specs=[hbm] * 11,
        out_specs=vmem,
        scratch_shapes=[
            pltpu.VMEM((SEQ, FEAT), BF16),
            pltpu.VMEM((1, QL), F32),
            pltpu.VMEM((1, LAT), F32),
            pltpu.VMEM((SEQ, 32), jnp.int32),
            pltpu.SMEM((1, SEQ), jnp.int32),
            pltpu.VMEM((FEAT, QL), BF16),
            pltpu.VMEM((FEAT, KW), BF16),
            pltpu.VMEM((QL, 2 * KW), BF16),
            pltpu.VMEM((2, LAT, HV), BF16),
            pltpu.VMEM((2 * HV, NC * FEAT), BF16),
            pltpu.VMEM((SEQ, KW, POS), BF16),
            pltpu.VMEM((NY, 3, SEQ, 128), F32),
            pltpu.VMEM((NY, 2, SEQ, 128), F32),
            pltpu.VMEM((NY - 1, 3, SEQ, 128), F32),
            pltpu.VMEM((NY - 1, 2, SEQ, 128), F32),
            pltpu.VMEM((3, SEQ, 128), F32),
            pltpu.VMEM((2, SEQ, 128), F32),
            pltpu.VMEM((NZ - 1, 3, SEQ, 128), F32),
            pltpu.VMEM((NZ - 1, 2, SEQ, 128), F32),
            pltpu.VMEM((NY, 3, SEQ, 128), F32),
            pltpu.VMEM((NY, SEQ, 128), F32),
            pltpu.VMEM((NC, 16, LAT), BF16),
            pltpu.VMEM((NZ, 2, 16, 128), BF16),
            pltpu.VMEM((NY, 16, 128), BF16),
            pltpu.VMEM((KT + 1, NC * 16, 128), F32),
            pltpu.VMEM((KT, NC * 16, 128), F32),
            pltpu.VMEM((NC * 16, 128), F32),
            pltpu.VMEM((NZ, NY, 16, LAT), BF16),
            pltpu.VMEM((len(GROUPS), NY, 16, 128), BF16),
            pltpu.VMEM((NZ, NY - 1, 16, LAT), BF16),
            pltpu.VMEM((len(GROUPS), NY - 1, 16, 128), BF16),
            pltpu.VMEM((NZ, 16, PADKW), BF16),
            pltpu.VMEM((NZ, 16, PADKW), BF16),
            pltpu.VMEM((max(1, len(DIRECT_SUM)) * NY, 16, PADKW), BF16),
            pltpu.VMEM((max(1, len(DIRECT_SUM)) * NY, 16, PADKW), BF16),
            pltpu.VMEM((NC, 16, 128), BF16),
            pltpu.VMEM((NC, 16, 128), BF16),
            pltpu.VMEM((16, 128), BF16),
            pltpu.VMEM((16, 128), BF16),
            dma((11,)),
            dma((16,)),
            dma((10,)),
            dma((NZ,)),
            dma((NZ,)),
            dma((NZ,)),
            dma((NZ,)),
            dma((len(GROUPS),)),
            pltpu.SemaphoreType.REGULAR,
        ],
        compiler_params=pltpu.CompilerParams(
            collective_id=0, has_side_effects=True, vmem_limit_bytes=60 << 20
        ),
        cost_estimate=pl.CostEstimate(
            flops=400_000_000, bytes_accessed=11_000_000, transcendentals=200_000
        ),
    )(*arrays)


def solution(mesh):
    return jax.shard_map(
        on_device,
        mesh=mesh,
        in_specs=(
            P("section", None, "cache"),
            P("section", "cache", None),
            P("section", "cache", None),
            P("section", None),
            P("section", None),
            P("section", None, "cache"),
            P("section", "cache", None, None),
            P("section", "cache", None),
            P("section", None, "cache", None),
            P("section", None, None),
            P("section", None),
        ),
        out_specs=P("section", None, "cache"),
        check_vma=False,
    )
```

```python
import functools

import jax
import jax.numpy as jnp
from jax import lax
from jax.experimental import pallas as pl
from jax.experimental.pallas import tpu as pltpu
from jax.sharding import PartitionSpec as P

MESH = pl.DeviceIdType.MESH
F32 = jnp.float32
BF16 = jnp.bfloat16

SEQ = 8
QL = 1536
LAT = 512
ROPE = 64
HV = 128
BLK = 64
KW = 576
PADKW = 640
NZ = 8
NY = 4
NC = NZ * NY
NSEC = 8
FEAT = 224
POS = 256
QT = QL // 128
KT = LAT // 128
SCALE = (HV + ROPE) ** (-0.5)
GROUPS = ((0, 1, 7, 2, 6, 3, 5, 4),)
DIRECT_Q = (1, 7, 2, 6)
DIRECT_SUM = (4, 1, 7)
SUM_ORDER = ((3, 5, 2, 6, 0),)
ORDER = sum(GROUPS, ())
STARTS = tuple(sum(len(group) for group in GROUPS[:g]) * NY * 16 for g in range(len(GROUPS)))
FAR_FIRST = (4, 3, 5, 2, 6, 1, 7, 0)


def split_three(value):
    high = value.astype(BF16).astype(F32)
    rest = value - high
    middle = rest.astype(BF16).astype(F32)
    return high, middle, rest - middle


def two_rows(value):
    high = value.astype(BF16)
    low = (value - high.astype(F32)).astype(BF16)
    return jnp.concatenate([high.astype(F32), low.astype(F32)], axis=0).astype(BF16)


def folded(value):
    half = value.shape[0] // 2
    return value[:half] + value[half:]


def stats_tile(top, total, places=0):
    lane = lax.broadcasted_iota(jnp.int32, (top.shape[0], 128), 1) - places
    stats = jnp.zeros((top.shape[0], 128), F32)
    for at, piece in enumerate(split_three(top) + split_three(total)):
        stats = jnp.where(lane == at, piece, stats)
    return stats


def read_stats(stats, place=0):
    lane = lax.broadcasted_iota(jnp.int32, stats.shape, 1) - place
    top = jnp.where((lane >= 0) & (lane < 3), stats, 0.0)
    total = jnp.where((lane >= 3) & (lane < 6), stats, 0.0)
    return jnp.sum(top, axis=1, keepdims=True), jnp.sum(total, axis=1, keepdims=True)


def merged(parts):
    top = functools.reduce(jnp.maximum, [p[1] for p in parts])
    scales = [jnp.exp(p[1] - top) for p in parts]
    total = functools.reduce(jnp.add, [p[2] * a for p, a in zip(parts, scales)])
    summed = functools.reduce(jnp.add, [p[0] * a for p, a in zip(parts, scales)])
    return summed, top, total


def kernel(
    hidden,
    query_down,
    latent_down,
    query_gain,
    latent_gain,
    query_up,
    value_up,
    output_proj,
    latent_cache,
    selected,
    lengths,
    out,
    hid,
    qgain,
    lgain,
    chosen,
    limits,
    qd,
    ld,
    qu,
    vu,
    op,
    kv,
    part_q,
    part_k,
    y_q,
    y_k,
    own_qs,
    own_ks,
    z_q,
    z_k,
    lat_q,
    lat_k,
    q_all,
    q_rope,
    r_in,
    q_f32,
    o_f32,
    s_f32,
    o_out,
    s_out,
    y_in,
    ys_in,
    c_out,
    z_in,
    f_out,
    f_in,
    e_out,
    e_in,
    x_out,
    x_in,
    load_sem,
    send_sem,
    recv_sem,
    qz_sem,
    qy_sem,
    rope_sem,
    dy_sem,
    ds_sem,
    next_sem,
    greet_sem,
):
    sec = lax.axis_index("section")
    me = lax.axis_index("cache")
    z = me // NY
    y = me % NY
    after = lax.rem(sec + 1, NSEC)
    before = lax.rem(sec + NSEC - 1, NSEC)

    def at(dz, dy):
        return {"cache": lax.rem(z + dz, NZ) * NY + lax.rem(y + dy, NY)}

    def load(source, target, index):
        copy = pltpu.make_async_copy(source, target, load_sem.at[index])
        copy.start()
        return copy

    def send(source, target, send_index, recv, device):
        pltpu.make_async_remote_copy(
            src_ref=source,
            dst_ref=target,
            send_sem=send_sem.at[send_index],
            recv_sem=recv,
            device_id=device,
            device_id_type=MESH,
        ).start()

    def wait_bytes(ref, sem):
        pltpu.make_async_copy(ref, ref, sem).wait()

    half = FEAT // 2
    hid_load = load(hidden.at[0], hid, 0)
    qd_loads = [
        load(query_down.at[0, pl.ds(k * half, half)], qd.at[pl.ds(k * half, half)], 1 + 10 * k)
        for k in range(2)
    ]
    barrier = pltpu.get_barrier_semaphore()
    for dz in (2, NZ - 2, 1, NZ - 1):
        pl.semaphore_signal(barrier, inc=1, device_id=at(dz, 0), device_id_type=MESH)
    for dy in (2, 1, 3):
        pl.semaphore_signal(barrier, inc=1, device_id=at(0, dy), device_id_type=MESH)
    for other in (after, before):
        pl.semaphore_signal(barrier, inc=1, device_id={"section": other}, device_id_type=MESH)

    ld_load = load(latent_down.at[0], ld, 2)
    qgain_load = load(query_gain, qgain, 3)
    lgain_load = load(latent_gain, lgain, 4)
    chosen_load = load(selected.at[0], chosen, 5)
    limits_load = load(lengths, limits, 6)

    hid_load.wait()
    rows = hid[...]
    for qd_load in qd_loads:
        qd_load.wait()
    qu_load = load(query_up.at[0], qu, 7)
    kv_load = load(latent_cache.at[0], kv, 8)
    vu_load = load(value_up.at[0], vu, 9)
    op_load = load(output_proj.at[0], op, 10)
    wide = jnp.dot(rows, qd[...], preferred_element_type=F32)
    for t in range(QT):
        part_q[t // 3, t % 3] = wide[:, t * 128 : (t + 1) * 128]

    pl.semaphore_wait(barrier, 4 + NY + 1)

    for dy in (2, 1, 3):
        chunk = part_q.at[lax.rem(y + dy, NY)]
        send(chunk, y_q.at[NY - 1 - dy], 0, recv_sem.at[0], at(0, dy))
    def greet(step):
        for dz in (2, NZ - 2):
            pl.semaphore_signal(
                greet_sem.at[step], inc=1, device_id=at(dz, 0), device_id_type=MESH
            )

    greet(0)
    ld_load.wait()
    wide = jnp.dot(rows, ld[...], preferred_element_type=F32)
    empty = jnp.zeros((SEQ, 128 - ROPE), F32)
    rope = jnp.concatenate([wide[:, LAT:], empty], axis=1)
    for t in range(KT):
        part_k[t, 0] = wide[:, t * 128 : (t + 1) * 128]
        part_k[t, 1] = rope
    for dy in (2, 1, 3):
        chunk = part_k.at[lax.rem(y + dy, NY)]
        send(chunk, y_k.at[NY - 1 - dy], 1, recv_sem.at[1], at(0, dy))
    own_rows = rows.astype(F32)
    right_rows = jnp.concatenate([own_rows[:, 128:], jnp.zeros((SEQ, 32), F32)], axis=1)
    x_out[...] = jnp.concatenate([own_rows[:, :128], right_rows], axis=0).astype(BF16)
    send(x_out, x_in, 2, recv_sem.at[2], {"section": after})

    pl.semaphore_wait(greet_sem.at[0], 2)
    wait_bytes(y_q, recv_sem.at[0])
    own_qs[...] = part_q[y] + y_q[0] + y_q[1] + y_q[2]
    for dz in (4, 3, 5, 2, 6, 1, 7):
        send(own_qs, z_q.at[NZ - 1 - dz], 3, recv_sem.at[3], at(dz, 0))
    wait_bytes(y_k, recv_sem.at[1])
    own_ks[...] = part_k[y] + y_k[0] + y_k[1] + y_k[2]
    for dz in (4, 3, 5, 2, 6, 1, 7):
        send(own_ks, z_k.at[NZ - 1 - dz], 4, recv_sem.at[4], at(dz, 0))

    wait_bytes(z_q, recv_sem.at[3])
    lat_q[y] = functools.reduce(jnp.add, [own_qs[...]] + [z_q[k] for k in range(NZ - 1)])
    for dy in (2, 1, 3):
        send(lat_q.at[y], lat_q.at[y], 5, recv_sem.at[5], at(0, dy))
    pl.semaphore_signal(next_sem, inc=1, device_id={"section": before}, device_id_type=MESH)
    wait_bytes(z_k, recv_sem.at[4])
    sums = functools.reduce(jnp.add, [own_ks[...]] + [z_k[k] for k in range(NZ - 1)])
    lat_k[y] = sums[0]
    new_rope = sums[1]
    for dy in (2, 1, 3):
        send(lat_k.at[y], lat_k.at[y], 6, recv_sem.at[6], at(0, dy))
    qgain_load.wait()
    qu_load.wait()
    wait_bytes(lat_q.at[pl.ds(0, NY - 1)], recv_sem.at[5])

    tiles = [lat_q[t // 3, t % 3] for t in range(QT)]
    squares = functools.reduce(jnp.add, [tile * tile for tile in tiles])
    mean = jnp.sum(squares, axis=1, keepdims=True) * (1.0 / QL)
    q_scale = lax.rsqrt(mean + 1e-06)
    query_norm = jnp.concatenate(
        [tiles[t] * q_scale * qgain[0:1, t * 128 : (t + 1) * 128] for t in range(QT)], axis=1
    ).astype(BF16)
    own = jnp.dot(query_norm, qu[...], preferred_element_type=F32)
    first = own[:, :PADKW]
    second = pltpu.roll(own[:, LAT:], PADKW - ROPE, axis=1)
    own_q = jnp.concatenate([first, second], axis=0).astype(BF16)
    q_all[0] = own_q[:, :LAT]
    lane = lax.broadcasted_iota(jnp.int32, (SEQ, 128), 1)
    pair = jnp.where(lane < ROPE, own[:, LAT : LAT + 128], own[:, 2 * KW - 128 :])
    r_in[0] = jnp.concatenate([pair, jnp.zeros((SEQ, 128), F32)], axis=0).astype(BF16)

    for dz in (4, 3, 5, 2, 6, 1, 7):
        r = NZ - dz
        if r in DIRECT_Q:
            for dy in (2, 1, 3, 0):
                target = q_all.at[r * NY + (NY - dy) % NY]
                send(q_all.at[0], target, 7, qy_sem.at[r], at(dz, dy))
        else:
            send(q_all.at[0], q_all.at[r * NY], 7, qz_sem.at[r], at(dz, 0))
    for dy in (2, 1, 3):
        send(r_in.at[0], r_in.at[NY - dy], 8, rope_sem.at[0], at(0, dy))
    for dy in (2, 1, 3):
        send(q_all.at[0], q_all.at[NY - dy], 9, qy_sem.at[0], at(0, dy))

    wait_bytes(lat_k.at[pl.ds(0, NY - 1)], recv_sem.at[6])
    lgain_load.wait()
    tiles = [lat_k[t] for t in range(KT)]
    squares = functools.reduce(jnp.add, [tile * tile for tile in tiles])
    mean = jnp.sum(squares, axis=1, keepdims=True) * (1.0 / LAT)
    kv_scale = lax.rsqrt(mean + 1e-06)
    new_key = jnp.concatenate(
        [tiles[t] * kv_scale * lgain[0:1, t * 128 : (t + 1) * 128] for t in range(KT)]
        + [new_rope],
        axis=1,
    )
    new_key = new_key.astype(BF16).astype(F32)
    new_key = jnp.concatenate([new_key, new_key], axis=0)
    new_score = jnp.sum(own_q.astype(F32) * new_key, axis=1, keepdims=True) * SCALE

    chosen_load.wait()
    picked = chosen[...]
    lane = lax.broadcasted_iota(jnp.int32, (SEQ, POS), 1)
    hits = jnp.zeros((SEQ, POS), F32)
    for j in range(POS // BLK):
        hit = jnp.where(picked == me * (POS // BLK) + j, 1.0, 0.0)
        hit = jnp.max(hit, axis=1, keepdims=True)
        hits = jnp.where(lane // BLK == j, hit, hits)
    position = lax.broadcasted_iota(jnp.int32, (1, POS), 1) + me * POS
    limits_load.wait()

    def forward(r):
        block = q_all.at[r * NY]
        wait_bytes(block, qz_sem.at[r])
        for dy in (2, 1, 3):
            target = q_all.at[r * NY + NY - dy]
            send(block, target, 9, qy_sem.at[r], at(0, dy))

    wait_bytes(r_in.at[pl.ds(0, NY - 1)], rope_sem.at[0])
    for k in range(2):
        two = [r_in[2 * k].astype(F32)[:SEQ], r_in[2 * k + 1].astype(F32)[:SEQ]]
        q_rope[0, k] = jnp.concatenate(two, axis=0).astype(BF16)
    for dz in (4, 3, 5, 2, 6, 1, 7):
        r = NZ - dz
        send(q_rope.at[0], q_rope.at[r], 10, rope_sem.at[r], at(dz, 0))
    for r in (1, 7, 2, 6, 3, 5, 4):
        if r not in DIRECT_Q:
            forward(r)

    kv_load.wait()

    def attend(g):
        base = STARTS[g]
        heads = len(GROUPS[g]) * NY * 2
        row = lax.broadcasted_iota(jnp.int32, (heads, 1), 0)
        places = row // (2 * NY) * 6
        for p, r in enumerate(GROUPS[g]):
            arriving = NY if r in DIRECT_Q else NY - 1
            wait_bytes(q_all.at[pl.ds(0, arriving)], qy_sem.at[r])
            if r > 0:
                wait_bytes(q_rope.at[r], rope_sem.at[r])
            for k in range(NY):
                rows_at = base + (p * NY + k) * 16
                block = q_all[r * NY + k].astype(F32)
                for t in range(KT):
                    q_f32[t, rows_at : rows_at + 16, :] = block[:, t * 128 : (t + 1) * 128]
            for k in range(2):
                two = q_rope[r, k].astype(F32)
                other = pltpu.roll(two, ROPE, axis=1)
                for m in range(2):
                    rows_at = base + (p * NY + 2 * k + m) * 16
                    own_rows = slice(m * SEQ, (m + 1) * SEQ)
                    q_f32[KT, rows_at : rows_at + SEQ, :] = two[own_rows]
                    q_f32[KT, rows_at + SEQ : rows_at + 16, :] = other[own_rows]
        for b in range(SEQ):
            queries = jnp.concatenate(
                [q_f32[t, pl.ds(base + b, heads, stride=SEQ), :] for t in range(KT + 1)],
                axis=1,
            )
            queries = queries[:, :KW].astype(BF16)
            keys = kv[b]
            scores = jnp.dot(queries, keys, preferred_element_type=F32) * SCALE
            valid = (hits[b : b + 1, :] > 0.5) & (position < limits[0, b])
            masked = jnp.where(valid, scores, -1e30)
            top = jnp.max(masked, axis=1, keepdims=True)
            expo = jnp.where(valid, jnp.exp(masked - top), 0.0)
            total = jnp.sum(expo, axis=1, keepdims=True)
            summed = folded(
                lax.dot_general(
                    two_rows(expo),
                    keys[:LAT],
                    (((1,), (1,)), ((), ())),
                    preferred_element_type=F32,
                )
            )
            rows_at = pl.ds(base + b, heads, stride=SEQ)
            for t in range(KT):
                o_f32[t, rows_at, :] = summed[:, t * 128 : (t + 1) * 128]
            s_f32[rows_at, :] = stats_tile(top, total, places)

    def rows_of(g, p, k):
        start = STARTS[g] + (p * NY + k) * 16
        return slice(start, start + 16)

    def sums_of(g, p, k):
        return jnp.concatenate([o_f32[t, rows_of(g, p, k), :] for t in range(KT)], axis=1)

    def send_sums(g):
        staged = [GROUPS[g].index(r) for r in SUM_ORDER[g]]
        for k in (2, 1, 3):
            stats = [s_f32[rows_of(g, p, k), :] for p in staged]
            s_out[g, k] = functools.reduce(jnp.add, stats).astype(BF16)
            send(s_out.at[g, k], ys_in.at[g, NY - 1 - k], 11, ds_sem.at[g], at(0, k))
        for r in SUM_ORDER[g]:
            p = GROUPS[g].index(r)
            for k in (2, 1, 3):
                o_out[r, k] = sums_of(g, p, k).astype(BF16)
                send(o_out.at[r, k], y_in.at[r, NY - 1 - k], 12, dy_sem.at[r], at(0, k))
        for f, r in enumerate(DIRECT_SUM):
            if r in GROUPS[g]:
                p = GROUPS[g].index(r)
                to = DIRECT_SUM.index(NZ - r) * NY
                for k in (2, 1, 3, 0):
                    stats = s_f32[rows_of(g, p, k), :]
                    stats = pltpu.roll(stats, (128 - 6 * p) % 128, axis=1) if p else stats
                    wide = jnp.concatenate([sums_of(g, p, k), stats], axis=1)
                    f_out[f * NY + k] = wide.astype(BF16)
                    target = f_in.at[to + (NY - k) % NY]
                    send(f_out.at[f * NY + k], target, 15, recv_sem.at[9], at(r, k))

    def join_sums(g):
        wait_bytes(ys_in.at[g], ds_sem.at[g])
        for r in SUM_ORDER[g]:
            p = GROUPS[g].index(r)
            wait_bytes(y_in.at[r], dy_sem.at[r])
            parts = [(sums_of(g, p, 0), *read_stats(s_f32[rows_of(g, p, 0), :], 6 * p))]
            for k in range(NY - 1):
                stats = read_stats(ys_in[g, k].astype(F32), 6 * p)
                parts.append((y_in[r, k].astype(F32), *stats))
            summed, top, total = merged(parts)
            if r == 0:
                return summed, top, total
            wide = jnp.concatenate([summed, stats_tile(top, total)], axis=1)
            c_out[r] = wide.astype(BF16)
            send(c_out.at[r], z_in.at[NZ - r], 13, recv_sem.at[7], at(r, 0))

    for g in range(len(GROUPS)):
        attend(g)
        send_sums(g)
    own_parts = [join_sums(g) for g in range(len(GROUPS))]
    parts = [part for part in own_parts if part is not None]
    parts.append((new_key[:, :LAT], new_score, jnp.ones((2 * SEQ, 1), F32)))

    def joined_with(parts, blocks):
        for block in blocks:
            block = block.astype(F32)
            parts = parts + [(block[:, :LAT], *read_stats(block[:, LAT:]))]
        return merged(parts)

    if DIRECT_SUM:
        wait_bytes(f_in, recv_sem.at[9])
        parts = [joined_with(parts, [f_in[k] for k in range(len(DIRECT_SUM) * NY)])]
    staged = sum(SUM_ORDER, ())
    wait_bytes(z_in.at[pl.ds(0, len(staged) - 1)], recv_sem.at[7])
    summed, _, total = joined_with(parts, [z_in[r] for r in range(1, NZ) if r in staged])
    attended = summed / total

    vu_load.wait()
    heads = []
    for h in range(2):
        both = two_rows(attended[h * SEQ : (h + 1) * SEQ, :])
        heads.append(folded(jnp.dot(both, vu[h], preferred_element_type=F32)))
    head_out = two_rows(jnp.concatenate(heads, axis=1))
    op_load.wait()
    pl.semaphore_wait(next_sem, 1)
    width = NY * FEAT
    for r in FAR_FIRST:
        zt = lax.rem(z + r, NZ)
        columns = op[:, pl.ds(pl.multiple_of(zt * width, 128), width)]
        projected = folded(jnp.dot(head_out, columns, preferred_element_type=F32))
        for k in range(NY):
            start = k * FEAT // 128 * 128
            shift = k * FEAT - start
            stop = -(-(k * FEAT + FEAT) // 128) * 128
            piece = projected[:, start:stop]
            if shift:
                piece = pltpu.roll(piece, stop - start - shift, axis=1)
            block = jnp.concatenate([piece[:, :128], piece[:, 128:256]], axis=0)
            e_out[r * NY + k] = block.astype(BF16)
            slot = (NZ - r) % NZ * NY + y
            target = {"section": after, "cache": zt * NY + k}
            send(e_out.at[r * NY + k], e_in.at[slot], 14, recv_sem.at[8], target)

    wait_bytes(x_in, recv_sem.at[2])
    total = x_in[...].astype(F32)
    wait_bytes(e_in, recv_sem.at[8])
    for slot in range(NC):
        total = total + e_in[slot].astype(F32)
    out[0, :, :128] = total[:SEQ]
    out[0, :, 128:] = total[SEQ:, : FEAT - 128]

    wait_bytes(y_q, send_sem.at[0])
    wait_bytes(y_k, send_sem.at[1])
    wait_bytes(x_out, send_sem.at[2])
    wait_bytes(z_q, send_sem.at[3])
    wait_bytes(z_k, send_sem.at[4])
    wait_bytes(lat_q.at[pl.ds(0, NY - 1)], send_sem.at[5])
    wait_bytes(lat_k.at[pl.ds(0, NY - 1)], send_sem.at[6])
    straight = len(DIRECT_Q)
    wait_bytes(q_all.at[pl.ds(0, NZ - 1 + (NY - 1) * straight)], send_sem.at[7])
    wait_bytes(r_in.at[pl.ds(0, NY - 1)], send_sem.at[8])
    wait_bytes(q_all.at[pl.ds(0, (NZ - straight) * (NY - 1))], send_sem.at[9])
    wait_bytes(q_rope.at[pl.ds(0, NZ - 1)], send_sem.at[10])
    wait_bytes(ys_in, send_sem.at[11])
    wait_bytes(y_in.at[pl.ds(0, len(staged))], send_sem.at[12])
    wait_bytes(z_in.at[pl.ds(0, len(staged) - 1)], send_sem.at[13])
    if DIRECT_SUM:
        wait_bytes(f_out, send_sem.at[15])
    wait_bytes(e_out, send_sem.at[14])


def on_device(*arrays):
    arrays = list(arrays)
    arrays[8] = jnp.swapaxes(arrays[8], 2, 3)
    vmem = pl.BlockSpec(memory_space=pltpu.VMEM)
    hbm = pl.BlockSpec(memory_space=pl.ANY)
    dma = pltpu.SemaphoreType.DMA
    return pl.pallas_call(
        kernel,
        out_shape=pltpu.VMEM((1, SEQ, FEAT), F32),
        in_specs=[hbm] * 11,
        out_specs=vmem,
        scratch_shapes=[
            pltpu.VMEM((SEQ, FEAT), BF16),
            pltpu.VMEM((1, QL), F32),
            pltpu.VMEM((1, LAT), F32),
            pltpu.VMEM((SEQ, 32), jnp.int32),
            pltpu.SMEM((1, SEQ), jnp.int32),
            pltpu.VMEM((FEAT, QL), BF16),
            pltpu.VMEM((FEAT, KW), BF16),
            pltpu.VMEM((QL, 2 * KW), BF16),
            pltpu.VMEM((2, LAT, HV), BF16),
            pltpu.VMEM((2 * HV, NC * FEAT), BF16),
            pltpu.VMEM((SEQ, KW, POS), BF16),
            pltpu.VMEM((NY, 3, SEQ, 128), F32),
            pltpu.VMEM((NY, 2, SEQ, 128), F32),
            pltpu.VMEM((NY - 1, 3, SEQ, 128), F32),
            pltpu.VMEM((NY - 1, 2, SEQ, 128), F32),
            pltpu.VMEM((3, SEQ, 128), F32),
            pltpu.VMEM((2, SEQ, 128), F32),
            pltpu.VMEM((NZ - 1, 3, SEQ, 128), F32),
            pltpu.VMEM((NZ - 1, 2, SEQ, 128), F32),
            pltpu.VMEM((NY, 3, SEQ, 128), F32),
            pltpu.VMEM((NY, SEQ, 128), F32),
            pltpu.VMEM((NC, 16, LAT), BF16),
            pltpu.VMEM((NZ, 2, 16, 128), BF16),
            pltpu.VMEM((NY, 16, 128), BF16),
            pltpu.VMEM((KT + 1, NC * 16, 128), F32),
            pltpu.VMEM((KT, NC * 16, 128), F32),
            pltpu.VMEM((NC * 16, 128), F32),
            pltpu.VMEM((NZ, NY, 16, LAT), BF16),
            pltpu.VMEM((len(GROUPS), NY, 16, 128), BF16),
            pltpu.VMEM((NZ, NY - 1, 16, LAT), BF16),
            pltpu.VMEM((len(GROUPS), NY - 1, 16, 128), BF16),
            pltpu.VMEM((NZ, 16, PADKW), BF16),
            pltpu.VMEM((NZ, 16, PADKW), BF16),
            pltpu.VMEM((max(1, len(DIRECT_SUM)) * NY, 16, PADKW), BF16),
            pltpu.VMEM((max(1, len(DIRECT_SUM)) * NY, 16, PADKW), BF16),
            pltpu.VMEM((NC, 16, 128), BF16),
            pltpu.VMEM((NC, 16, 128), BF16),
            pltpu.VMEM((16, 128), BF16),
            pltpu.VMEM((16, 128), BF16),
            dma((12,)),
            dma((16,)),
            dma((10,)),
            dma((NZ,)),
            dma((NZ,)),
            dma((NZ,)),
            dma((NZ,)),
            dma((len(GROUPS),)),
            pltpu.SemaphoreType.REGULAR,
            pltpu.SemaphoreType.REGULAR((1,)),
        ],
        compiler_params=pltpu.CompilerParams(
            collective_id=0, has_side_effects=True, vmem_limit_bytes=60 << 20
        ),
        cost_estimate=pl.CostEstimate(
            flops=400_000_000, bytes_accessed=11_000_000, transcendentals=200_000
        ),
    )(*arrays)


def solution(mesh):
    return jax.shard_map(
        on_device,
        mesh=mesh,
        in_specs=(
            P("section", None, "cache"),
            P("section", "cache", None),
            P("section", "cache", None),
            P("section", None),
            P("section", None),
            P("section", None, "cache"),
            P("section", "cache", None, None),
            P("section", "cache", None),
            P("section", None, "cache", None),
            P("section", None, None),
            P("section", None),
        ),
        out_specs=P("section", None, "cache"),
        check_vma=False,
    )
```

```python
import functools

import jax
import jax.numpy as jnp
from jax import lax
from jax.experimental import pallas as pl
from jax.experimental.pallas import tpu as pltpu
from jax.sharding import PartitionSpec as P

MESH = pl.DeviceIdType.MESH
F32 = jnp.float32
BF16 = jnp.bfloat16

SEQ = 8
QL = 1536
LAT = 512
ROPE = 64
HV = 128
BLK = 64
KW = 576
PADKW = 640
NZ = 8
NY = 4
NC = NZ * NY
NSEC = 8
FEAT = 224
POS = 256
QT = QL // 128
KT = LAT // 128
SCALE = (HV + ROPE) ** (-0.5)
GROUPS = ((0, 1, 7, 2, 6, 3, 5, 4),)
DIRECT_Q = (1, 7, 2, 6)
DIRECT_SUM = (4, 1, 7)
SUM_ORDER = ((3, 5, 2, 6, 0),)
ORDER = sum(GROUPS, ())
STARTS = tuple(sum(len(group) for group in GROUPS[:g]) * NY * 16 for g in range(len(GROUPS)))
FAR_FIRST = (4, 3, 5, 2, 6, 1, 7, 0)


def split_three(value):
    high = value.astype(BF16).astype(F32)
    rest = value - high
    middle = rest.astype(BF16).astype(F32)
    return high, middle, rest - middle


def two_rows(value):
    high = value.astype(BF16)
    low = (value - high.astype(F32)).astype(BF16)
    return jnp.concatenate([high.astype(F32), low.astype(F32)], axis=0).astype(BF16)


def folded(value):
    half = value.shape[0] // 2
    return value[:half] + value[half:]


def stats_tile(top, total, places=0):
    lane = lax.broadcasted_iota(jnp.int32, (top.shape[0], 128), 1) - places
    stats = jnp.zeros((top.shape[0], 128), F32)
    for at, piece in enumerate(split_three(top) + split_three(total)):
        stats = jnp.where(lane == at, piece, stats)
    return stats


def read_stats(stats, place=0):
    lane = lax.broadcasted_iota(jnp.int32, stats.shape, 1) - place
    top = jnp.where((lane >= 0) & (lane < 3), stats, 0.0)
    total = jnp.where((lane >= 3) & (lane < 6), stats, 0.0)
    return jnp.sum(top, axis=1, keepdims=True), jnp.sum(total, axis=1, keepdims=True)


def pack(block, summed, stats, place=0):
    for t in range(KT):
        columns = slice(t * 128, (t + 1) * 128)
        block[t] = summed[:SEQ, columns].astype(BF16)
        block[KT + t] = summed[SEQ:, columns].astype(BF16)
    upper = pltpu.roll(stats[:SEQ], 128 - place, axis=1) if place else stats[:SEQ]
    lower = pltpu.roll(stats[SEQ:], 64 - place, axis=1)
    block[2 * KT] = (upper + lower).astype(BF16)


def unpack(block):
    tiles = [block[t].astype(F32) for t in range(2 * KT + 1)]
    upper = jnp.concatenate(tiles[:KT], axis=1)
    lower = jnp.concatenate(tiles[KT : 2 * KT], axis=1)
    stats = jnp.concatenate([tiles[-1], pltpu.roll(tiles[-1], 64, axis=1)], axis=0)
    return jnp.concatenate([upper, lower], axis=0), *read_stats(stats)


def merged(parts):
    top = functools.reduce(jnp.maximum, [p[1] for p in parts])
    scales = [jnp.exp(p[1] - top) for p in parts]
    total = functools.reduce(jnp.add, [p[2] * a for p, a in zip(parts, scales)])
    summed = functools.reduce(jnp.add, [p[0] * a for p, a in zip(parts, scales)])
    return summed, top, total


def kernel(
    hidden,
    query_down,
    latent_down,
    query_gain,
    latent_gain,
    query_up,
    value_up,
    output_proj,
    latent_cache,
    selected,
    lengths,
    out,
    hid,
    qgain,
    lgain,
    chosen,
    limits,
    qd,
    ld,
    qu,
    vu,
    op,
    kv,
    part_q,
    part_k,
    y_q,
    y_k,
    own_qs,
    own_ks,
    z_q,
    z_k,
    lat_q,
    lat_k,
    q_all,
    q_f32,
    o_f32,
    s_f32,
    o_out,
    s_out,
    y_in,
    ys_in,
    c_out,
    z_in,
    f_out,
    f_in,
    e_out,
    e_in,
    x_out,
    x_in,
    load_sem,
    send_sem,
    recv_sem,
    qz_sem,
    qy_sem,
    dy_sem,
    ds_sem,
    next_sem,
    greet_sem,
):
    sec = lax.axis_index("section")
    me = lax.axis_index("cache")
    z = me // NY
    y = me % NY
    after = lax.rem(sec + 1, NSEC)
    before = lax.rem(sec + NSEC - 1, NSEC)

    def at(dz, dy):
        return {"cache": lax.rem(z + dz, NZ) * NY + lax.rem(y + dy, NY)}

    def load(source, target, index):
        copy = pltpu.make_async_copy(source, target, load_sem.at[index])
        copy.start()
        return copy

    def send(source, target, send_index, recv, device):
        pltpu.make_async_remote_copy(
            src_ref=source,
            dst_ref=target,
            send_sem=send_sem.at[send_index],
            recv_sem=recv,
            device_id=device,
            device_id_type=MESH,
        ).start()

    def wait_bytes(ref, sem):
        pltpu.make_async_copy(ref, ref, sem).wait()

    half = FEAT // 2
    hid_load = load(hidden.at[0], hid, 0)
    qd_loads = [
        load(query_down.at[0, pl.ds(k * half, half)], qd.at[pl.ds(k * half, half)], 1 + 10 * k)
        for k in range(2)
    ]
    barrier = pltpu.get_barrier_semaphore()
    for dz in (2, NZ - 2, 1, NZ - 1):
        pl.semaphore_signal(barrier, inc=1, device_id=at(dz, 0), device_id_type=MESH)
    for dy in (2, 1, 3):
        pl.semaphore_signal(barrier, inc=1, device_id=at(0, dy), device_id_type=MESH)
    for other in (after, before):
        pl.semaphore_signal(barrier, inc=1, device_id={"section": other}, device_id_type=MESH)

    ld_load = load(latent_down.at[0], ld, 2)
    qgain_load = load(query_gain, qgain, 3)
    lgain_load = load(latent_gain, lgain, 4)
    chosen_load = load(selected.at[0], chosen, 5)
    limits_load = load(lengths, limits, 6)

    hid_load.wait()
    rows = hid[...]
    for qd_load in qd_loads:
        qd_load.wait()
    qu_load = load(query_up.at[0], qu, 7)
    kv_load = load(latent_cache.at[0], kv, 8)
    vu_load = load(value_up.at[0], vu, 9)
    op_load = load(output_proj.at[0], op, 10)
    wide = jnp.dot(rows, qd[...], preferred_element_type=F32)
    for t in range(QT):
        part_q[t // 3, t % 3] = wide[:, t * 128 : (t + 1) * 128]

    pl.semaphore_wait(barrier, 4 + NY + 1)

    for dy in (2, 1, 3):
        chunk = part_q.at[lax.rem(y + dy, NY)]
        send(chunk, y_q.at[NY - 1 - dy], 0, recv_sem.at[0], at(0, dy))
    def greet(step):
        for dz in (2, NZ - 2):
            pl.semaphore_signal(
                greet_sem.at[step], inc=1, device_id=at(dz, 0), device_id_type=MESH
            )

    greet(0)
    ld_load.wait()
    wide = jnp.dot(rows, ld[...], preferred_element_type=F32)
    empty = jnp.zeros((SEQ, 128 - ROPE), F32)
    rope = jnp.concatenate([wide[:, LAT:], empty], axis=1)
    for t in range(KT):
        part_k[t, 0] = wide[:, t * 128 : (t + 1) * 128]
        part_k[t, 1] = rope
    for dy in (2, 1, 3):
        chunk = part_k.at[lax.rem(y + dy, NY)]
        send(chunk, y_k.at[NY - 1 - dy], 1, recv_sem.at[1], at(0, dy))
    own_rows = rows.astype(F32)
    right_rows = jnp.concatenate([own_rows[:, 128:], jnp.zeros((SEQ, 32), F32)], axis=1)
    x_out[...] = jnp.concatenate([own_rows[:, :128], right_rows], axis=0).astype(BF16)
    send(x_out, x_in, 2, recv_sem.at[2], {"section": after})

    pl.semaphore_wait(greet_sem.at[0], 2)
    wait_bytes(y_q, recv_sem.at[0])
    own_qs[...] = part_q[y] + y_q[0] + y_q[1] + y_q[2]
    for dz in (4, 3, 5, 2, 6, 1, 7):
        send(own_qs, z_q.at[NZ - 1 - dz], 3, recv_sem.at[3], at(dz, 0))
    wait_bytes(y_k, recv_sem.at[1])
    own_ks[...] = part_k[y] + y_k[0] + y_k[1] + y_k[2]
    for dz in (4, 3, 5, 2, 6, 1, 7):
        send(own_ks, z_k.at[NZ - 1 - dz], 4, recv_sem.at[4], at(dz, 0))

    wait_bytes(z_q, recv_sem.at[3])
    lat_q[y] = functools.reduce(jnp.add, [own_qs[...]] + [z_q[k] for k in range(NZ - 1)])
    for dy in (2, 1, 3):
        send(lat_q.at[y], lat_q.at[y], 5, recv_sem.at[5], at(0, dy))
    pl.semaphore_signal(next_sem, inc=1, device_id={"section": before}, device_id_type=MESH)
    wait_bytes(z_k, recv_sem.at[4])
    sums = functools.reduce(jnp.add, [own_ks[...]] + [z_k[k] for k in range(NZ - 1)])
    lat_k[y] = sums[0]
    new_rope = sums[1]
    for dy in (2, 1, 3):
        send(lat_k.at[y], lat_k.at[y], 6, recv_sem.at[6], at(0, dy))
    qgain_load.wait()
    qu_load.wait()
    wait_bytes(lat_q.at[pl.ds(0, NY - 1)], recv_sem.at[5])

    tiles = [lat_q[t // 3, t % 3] for t in range(QT)]
    squares = functools.reduce(jnp.add, [tile * tile for tile in tiles])
    mean = jnp.sum(squares, axis=1, keepdims=True) * (1.0 / QL)
    q_scale = lax.rsqrt(mean + 1e-06)
    query_norm = jnp.concatenate(
        [tiles[t] * q_scale * qgain[0:1, t * 128 : (t + 1) * 128] for t in range(QT)], axis=1
    ).astype(BF16)
    own = jnp.dot(query_norm, qu[...], preferred_element_type=F32)
    first = own[:, :PADKW]
    second = pltpu.roll(own[:, LAT:], PADKW - ROPE, axis=1)
    own_q = jnp.concatenate([first, second], axis=0).astype(BF16)
    for t in range(KT):
        q_all[0, t] = first[:, t * 128 : (t + 1) * 128].astype(BF16)
        q_all[0, KT + t] = second[:, t * 128 : (t + 1) * 128].astype(BF16)
    lane = lax.broadcasted_iota(jnp.int32, (SEQ, 128), 1)
    pair = jnp.where(lane < ROPE, own[:, LAT : LAT + 128], own[:, 2 * KW - 128 :])
    q_all[0, 2 * KT] = pair.astype(BF16)

    for dz in (4, 3, 5, 2, 6, 1, 7):
        r = NZ - dz
        if r in DIRECT_Q:
            for dy in (2, 1, 3, 0):
                target = q_all.at[r * NY + (NY - dy) % NY]
                send(q_all.at[0], target, 7, qy_sem.at[r], at(dz, dy))
        else:
            send(q_all.at[0], q_all.at[r * NY], 7, qz_sem.at[r], at(dz, 0))
    for dy in (2, 1, 3):
        send(q_all.at[0], q_all.at[NY - dy], 8, qy_sem.at[0], at(0, dy))

    wait_bytes(lat_k.at[pl.ds(0, NY - 1)], recv_sem.at[6])
    lgain_load.wait()
    tiles = [lat_k[t] for t in range(KT)]
    squares = functools.reduce(jnp.add, [tile * tile for tile in tiles])
    mean = jnp.sum(squares, axis=1, keepdims=True) * (1.0 / LAT)
    kv_scale = lax.rsqrt(mean + 1e-06)
    new_key = jnp.concatenate(
        [tiles[t] * kv_scale * lgain[0:1, t * 128 : (t + 1) * 128] for t in range(KT)]
        + [new_rope],
        axis=1,
    )
    new_key = new_key.astype(BF16).astype(F32)
    new_key = jnp.concatenate([new_key, new_key], axis=0)
    new_score = jnp.sum(own_q.astype(F32) * new_key, axis=1, keepdims=True) * SCALE

    chosen_load.wait()
    picked = chosen[...]
    lane = lax.broadcasted_iota(jnp.int32, (SEQ, POS), 1)
    hits = jnp.zeros((SEQ, POS), F32)
    for j in range(POS // BLK):
        hit = jnp.where(picked == me * (POS // BLK) + j, 1.0, 0.0)
        hit = jnp.max(hit, axis=1, keepdims=True)
        hits = jnp.where(lane // BLK == j, hit, hits)
    position = lax.broadcasted_iota(jnp.int32, (1, POS), 1) + me * POS
    limits_load.wait()

    def forward(r):
        block = q_all.at[r * NY]
        wait_bytes(block, qz_sem.at[r])
        for dy in (2, 1, 3):
            target = q_all.at[r * NY + NY - dy]
            send(block, target, 8, qy_sem.at[r], at(0, dy))

    for r in (1, 7, 2, 6, 3, 5, 4):
        if r not in DIRECT_Q:
            forward(r)

    kv_load.wait()

    def attend(g):
        base = STARTS[g]
        heads = len(GROUPS[g]) * NY * 2
        row = lax.broadcasted_iota(jnp.int32, (heads, 1), 0)
        places = row // (2 * NY) * 6
        for p, r in enumerate(GROUPS[g]):
            arriving = NY if r in DIRECT_Q else NY - 1
            wait_bytes(q_all.at[pl.ds(0, arriving)], qy_sem.at[r])
            for k in range(NY):
                top_at = base + (p * NY + k) * 16
                low_at = top_at + SEQ
                block = q_all.at[r * NY + k]
                for t in range(KT):
                    q_f32[t, top_at : top_at + SEQ, :] = block[t].astype(F32)
                    q_f32[t, low_at : low_at + SEQ, :] = block[KT + t].astype(F32)
                pair = block[2 * KT].astype(F32)
                q_f32[KT, top_at : top_at + SEQ, :] = pair
                q_f32[KT, low_at : low_at + SEQ, :] = pltpu.roll(pair, ROPE, axis=1)
        for b in range(SEQ):
            queries = jnp.concatenate(
                [q_f32[t, pl.ds(base + b, heads, stride=SEQ), :] for t in range(KT + 1)],
                axis=1,
            )
            queries = queries[:, :KW].astype(BF16)
            keys = kv[b]
            scores = jnp.dot(queries, keys, preferred_element_type=F32) * SCALE
            valid = (hits[b : b + 1, :] > 0.5) & (position < limits[0, b])
            masked = jnp.where(valid, scores, -1e30)
            top = jnp.max(masked, axis=1, keepdims=True)
            expo = jnp.where(valid, jnp.exp(masked - top), 0.0)
            total = jnp.sum(expo, axis=1, keepdims=True)
            summed = folded(
                lax.dot_general(
                    two_rows(expo),
                    keys[:LAT],
                    (((1,), (1,)), ((), ())),
                    preferred_element_type=F32,
                )
            )
            rows_at = pl.ds(base + b, heads, stride=SEQ)
            for t in range(KT):
                o_f32[t, rows_at, :] = summed[:, t * 128 : (t + 1) * 128]
            s_f32[rows_at, :] = stats_tile(top, total, places)

    def rows_of(g, p, k):
        start = STARTS[g] + (p * NY + k) * 16
        return slice(start, start + 16)

    def sums_of(g, p, k):
        return jnp.concatenate([o_f32[t, rows_of(g, p, k), :] for t in range(KT)], axis=1)

    def send_sums(g):
        staged = [GROUPS[g].index(r) for r in SUM_ORDER[g]]
        for k in (2, 1, 3):
            stats = [s_f32[rows_of(g, p, k), :] for p in staged]
            s_out[g, k] = functools.reduce(jnp.add, stats).astype(BF16)
            send(s_out.at[g, k], ys_in.at[g, NY - 1 - k], 9, ds_sem.at[g], at(0, k))
        for r in SUM_ORDER[g]:
            p = GROUPS[g].index(r)
            for k in (2, 1, 3):
                o_out[r, k] = sums_of(g, p, k).astype(BF16)
                send(o_out.at[r, k], y_in.at[r, NY - 1 - k], 10, dy_sem.at[r], at(0, k))
        for f, r in enumerate(DIRECT_SUM):
            if r in GROUPS[g]:
                p = GROUPS[g].index(r)
                to = DIRECT_SUM.index(NZ - r) * NY
                for k in (2, 1, 3, 0):
                    stats = s_f32[rows_of(g, p, k), :]
                    pack(f_out.at[f * NY + k], sums_of(g, p, k), stats, 6 * p)
                    target = f_in.at[to + (NY - k) % NY]
                    send(f_out.at[f * NY + k], target, 13, recv_sem.at[9], at(r, k))

    def join_sums(g):
        wait_bytes(ys_in.at[g], ds_sem.at[g])
        for r in SUM_ORDER[g]:
            p = GROUPS[g].index(r)
            wait_bytes(y_in.at[r], dy_sem.at[r])
            parts = [(sums_of(g, p, 0), *read_stats(s_f32[rows_of(g, p, 0), :], 6 * p))]
            for k in range(NY - 1):
                stats = read_stats(ys_in[g, k].astype(F32), 6 * p)
                parts.append((y_in[r, k].astype(F32), *stats))
            summed, top, total = merged(parts)
            if r == 0:
                return summed, top, total
            pack(c_out.at[r], summed, stats_tile(top, total))
            send(c_out.at[r], z_in.at[NZ - r], 11, recv_sem.at[7], at(r, 0))

    for g in range(len(GROUPS)):
        attend(g)
        send_sums(g)
    own_parts = [join_sums(g) for g in range(len(GROUPS))]
    parts = [part for part in own_parts if part is not None]
    parts.append((new_key[:, :LAT], new_score, jnp.ones((2 * SEQ, 1), F32)))

    def joined_with(parts, blocks):
        return merged(parts + [unpack(block) for block in blocks])

    if DIRECT_SUM:
        wait_bytes(f_in, recv_sem.at[9])
        parts = [joined_with(parts, [f_in.at[k] for k in range(len(DIRECT_SUM) * NY)])]
    staged = sum(SUM_ORDER, ())
    wait_bytes(z_in.at[pl.ds(0, len(staged) - 1)], recv_sem.at[7])
    summed, _, total = joined_with(parts, [z_in.at[r] for r in range(1, NZ) if r in staged])
    attended = summed / total

    vu_load.wait()
    heads = []
    for h in range(2):
        both = two_rows(attended[h * SEQ : (h + 1) * SEQ, :])
        heads.append(folded(jnp.dot(both, vu[h], preferred_element_type=F32)))
    head_out = two_rows(jnp.concatenate(heads, axis=1))
    op_load.wait()
    pl.semaphore_wait(next_sem, 1)
    width = NY * FEAT
    for r in FAR_FIRST:
        zt = lax.rem(z + r, NZ)
        columns = op[:, pl.ds(pl.multiple_of(zt * width, 128), width)]
        projected = folded(jnp.dot(head_out, columns, preferred_element_type=F32))
        for k in range(NY):
            start = k * FEAT // 128 * 128
            shift = k * FEAT - start
            stop = -(-(k * FEAT + FEAT) // 128) * 128
            piece = projected[:, start:stop]
            if shift:
                piece = pltpu.roll(piece, stop - start - shift, axis=1)
            block = jnp.concatenate([piece[:, :128], piece[:, 128:256]], axis=0)
            e_out[r * NY + k] = block.astype(BF16)
            slot = (NZ - r) % NZ * NY + y
            target = {"section": after, "cache": zt * NY + k}
            send(e_out.at[r * NY + k], e_in.at[slot], 12, recv_sem.at[8], target)

    wait_bytes(x_in, recv_sem.at[2])
    total = x_in[...].astype(F32)
    wait_bytes(e_in, recv_sem.at[8])
    for slot in range(NC):
        total = total + e_in[slot].astype(F32)
    out[0, :, :128] = total[:SEQ]
    out[0, :, 128:] = total[SEQ:, : FEAT - 128]

    wait_bytes(y_q, send_sem.at[0])
    wait_bytes(y_k, send_sem.at[1])
    wait_bytes(x_out, send_sem.at[2])
    wait_bytes(z_q, send_sem.at[3])
    wait_bytes(z_k, send_sem.at[4])
    wait_bytes(lat_q.at[pl.ds(0, NY - 1)], send_sem.at[5])
    wait_bytes(lat_k.at[pl.ds(0, NY - 1)], send_sem.at[6])
    straight = len(DIRECT_Q)
    wait_bytes(q_all.at[pl.ds(0, NZ - 1 + (NY - 1) * straight)], send_sem.at[7])
    wait_bytes(q_all.at[pl.ds(0, (NZ - straight) * (NY - 1))], send_sem.at[8])
    wait_bytes(ys_in, send_sem.at[9])
    wait_bytes(y_in.at[pl.ds(0, len(staged))], send_sem.at[10])
    wait_bytes(z_in.at[pl.ds(0, len(staged) - 1)], send_sem.at[11])
    if DIRECT_SUM:
        wait_bytes(f_out, send_sem.at[13])
    wait_bytes(e_out, send_sem.at[12])


def on_device(*arrays):
    arrays = list(arrays)
    arrays[8] = jnp.swapaxes(arrays[8], 2, 3)
    vmem = pl.BlockSpec(memory_space=pltpu.VMEM)
    hbm = pl.BlockSpec(memory_space=pl.ANY)
    dma = pltpu.SemaphoreType.DMA
    return pl.pallas_call(
        kernel,
        out_shape=pltpu.VMEM((1, SEQ, FEAT), F32),
        in_specs=[hbm] * 11,
        out_specs=vmem,
        scratch_shapes=[
            pltpu.VMEM((SEQ, FEAT), BF16),
            pltpu.VMEM((1, QL), F32),
            pltpu.VMEM((1, LAT), F32),
            pltpu.VMEM((SEQ, 32), jnp.int32),
            pltpu.SMEM((1, SEQ), jnp.int32),
            pltpu.VMEM((FEAT, QL), BF16),
            pltpu.VMEM((FEAT, KW), BF16),
            pltpu.VMEM((QL, 2 * KW), BF16),
            pltpu.VMEM((2, LAT, HV), BF16),
            pltpu.VMEM((2 * HV, NC * FEAT), BF16),
            pltpu.VMEM((SEQ, KW, POS), BF16),
            pltpu.VMEM((NY, 3, SEQ, 128), F32),
            pltpu.VMEM((NY, 2, SEQ, 128), F32),
            pltpu.VMEM((NY - 1, 3, SEQ, 128), F32),
            pltpu.VMEM((NY - 1, 2, SEQ, 128), F32),
            pltpu.VMEM((3, SEQ, 128), F32),
            pltpu.VMEM((2, SEQ, 128), F32),
            pltpu.VMEM((NZ - 1, 3, SEQ, 128), F32),
            pltpu.VMEM((NZ - 1, 2, SEQ, 128), F32),
            pltpu.VMEM((NY, 3, SEQ, 128), F32),
            pltpu.VMEM((NY, SEQ, 128), F32),
            pltpu.VMEM((NC, 2 * KT + 1, SEQ, 128), BF16),
            pltpu.VMEM((KT + 1, NC * 16, 128), F32),
            pltpu.VMEM((KT, NC * 16, 128), F32),
            pltpu.VMEM((NC * 16, 128), F32),
            pltpu.VMEM((NZ, NY, 16, LAT), BF16),
            pltpu.VMEM((len(GROUPS), NY, 16, 128), BF16),
            pltpu.VMEM((NZ, NY - 1, 16, LAT), BF16),
            pltpu.VMEM((len(GROUPS), NY - 1, 16, 128), BF16),
            pltpu.VMEM((NZ, 2 * KT + 1, SEQ, 128), BF16),
            pltpu.VMEM((NZ, 2 * KT + 1, SEQ, 128), BF16),
            pltpu.VMEM((max(1, len(DIRECT_SUM)) * NY, 2 * KT + 1, SEQ, 128), BF16),
            pltpu.VMEM((max(1, len(DIRECT_SUM)) * NY, 2 * KT + 1, SEQ, 128), BF16),
            pltpu.VMEM((NC, 16, 128), BF16),
            pltpu.VMEM((NC, 16, 128), BF16),
            pltpu.VMEM((16, 128), BF16),
            pltpu.VMEM((16, 128), BF16),
            dma((12,)),
            dma((16,)),
            dma((10,)),
            dma((NZ,)),
            dma((NZ,)),
            dma((NZ,)),
            dma((len(GROUPS),)),
            pltpu.SemaphoreType.REGULAR,
            pltpu.SemaphoreType.REGULAR((1,)),
        ],
        compiler_params=pltpu.CompilerParams(
            collective_id=0, has_side_effects=True, vmem_limit_bytes=60 << 20
        ),
        cost_estimate=pl.CostEstimate(
            flops=400_000_000, bytes_accessed=11_000_000, transcendentals=200_000
        ),
    )(*arrays)


def solution(mesh):
    return jax.shard_map(
        on_device,
        mesh=mesh,
        in_specs=(
            P("section", None, "cache"),
            P("section", "cache", None),
            P("section", "cache", None),
            P("section", None),
            P("section", None),
            P("section", None, "cache"),
            P("section", "cache", None, None),
            P("section", "cache", None),
            P("section", None, "cache", None),
            P("section", None, None),
            P("section", None),
        ),
        out_specs=P("section", None, "cache"),
        check_vma=False,
    )
```
